512 devices in a mesh: pages: 64 (over y, x, core), heads: 8 (over z).
Axes of the slice: x: 4, y: 8, z: 8, core: 2. Of those that a mesh axis runs over, the one named last changes fastest.
Arguments:
- prefill_latent: bfloat16 [512, 64, 576], P('pages'), may hold values from -6 to 6
- stretch_page: int32 [512], replicated, may hold values from 0 to 511, as said below
- page_table: int32 [512, 2], replicated, may hold values from 0 to 63, as said below
- page_list: int32 [64, 64], replicated, may hold values from 0 to 511, as said below
- lengths: int32 [64], replicated, may hold values from 64 to 4096, as said below
- queries: bfloat16 [2, 64, 2, 128, 576], P(None, 'pages', None, 'heads'), may hold values from -64 to 64
- new_latent: bfloat16 [2, 64, 2, 576], P(None, 'pages'), may hold values from -24 to 24
Outputs:
- attended: bfloat16 [2, 64, 2, 128, 512], P(None, 'pages', None, 'heads')
- cache_pool: bfloat16 [512, 64, 576], P('pages', 'heads')
The draws below stay inside these ranges and needn't reach their ends.
Inputs may be any that keep to these rules, and one draw needn't show every extreme that they name: `page_table`: page j lies on owner (j + a) mod 64 for one a of each draw; each owner's 8 slots hold different pages. `stretch_page`: stretches d * 8 to (d + 1) * 8 - 1 name two runs of half of 8 consecutive logical pages, runs b and 127 - b for a b of their own; every logical page once. `page_list`: each row names 64 consecutive logical pages. `lengths`: some request reads all of its list.
All inputs are finite; a program needn't handle non-finite values.
Results may differ from the reference program's by a relative error of at most 0.0022.
Values may be sent and summed in bfloat16 or wider, within the bound.
A program may use at most 64 MiB of HBM per device.

```python
import jax
import jax.numpy as jnp
from jax import lax

LAT = 512
HEADS = 128
LATW = 576
PAGE = 64
ROWS = 2
STEPS = 2
SLOTS = 8
CAPR = 1
REQ = 64
PROMPT_PAGES = 512
MAXP = 64
N_PAGES = 64


SOFTMAX_SCALE = 192.0 ** (-0.5)


def fresh_base(key, rope_scale, rope_tie):
    latent_rows = jax.random.normal(key, (STEPS, REQ, ROWS, LATW), jnp.float32)
    latent_part = latent_rows[..., :LAT]
    rope_part = latent_rows[..., LAT:] * rope_scale
    first_rope = jnp.broadcast_to(rope_part[:, :, :1], rope_part.shape)
    rope_part = rope_part + rope_tie * (first_rope - rope_part)
    return jnp.clip(jnp.concatenate([latent_part, rope_part], axis=-1), -24.0, 24.0)


def draw_prefill_latent(key, part):
    key = jax.random.fold_in(key, 13)
    latent_rows = jax.random.normal(key, (PROMPT_PAGES, PAGE, LATW), jnp.float32)
    return jnp.clip(latent_rows, -6.0, 6.0).astype(jnp.bfloat16)


def draw_new_latent(key, part):
    base_rows = fresh_base(key, 1.0, 0.0)
    return base_rows.astype(jnp.bfloat16)


def draw_queries(key, part):
    base_rows = fresh_base(key, 1.0, 0.0)
    key = jax.random.fold_in(key, 23)
    noise_key, gain_key, strong_key = jax.random.split(key, 3)
    noise = jax.random.normal(noise_key, (STEPS, REQ, ROWS, HEADS, LATW), jnp.float32)
    target = jax.random.uniform(gain_key, (STEPS, REQ, ROWS, HEADS, 1), jnp.float32, 6.0, 12.0)
    aligned = noise + target / (LATW * SOFTMAX_SCALE) * base_rows[:, :, :, None, :]
    return jnp.clip(aligned, -64.0, 64.0).astype(jnp.bfloat16)


def draw_page_table(key, part):
    key = jax.random.fold_in(key, 31)
    shift_key, slot_key = jax.random.split(key)
    shift_amount = jax.random.randint(shift_key, (), 0, N_PAGES)
    page_ids = jnp.arange(PROMPT_PAGES, dtype=jnp.int32)
    owners = jnp.mod(page_ids + shift_amount, N_PAGES).astype(jnp.int32)
    rounds = (page_ids // N_PAGES).astype(jnp.int32)
    orders = jax.vmap(lambda k: jax.random.permutation(k, SLOTS))(jax.random.split(slot_key, N_PAGES)).astype(jnp.int32)
    places = orders[owners, rounds]
    return jnp.stack([owners, places], axis=1).astype(jnp.int32)


def draw_stretch_page(key, part):
    key = jax.random.fold_in(key, 47)
    blocks = jax.random.permutation(key, N_PAGES).astype(jnp.int32)
    half_run = SLOTS // 2
    stretch_ids = jnp.arange(PROMPT_PAGES, dtype=jnp.int32)
    device = stretch_ids // SLOTS
    within = stretch_ids % SLOTS
    first_block = blocks[device]
    run_block = jnp.where(within < half_run, first_block, 2 * N_PAGES - 1 - first_block)
    return (run_block * half_run + within % half_run).astype(jnp.int32)


def draw_page_list(key, part):
    key = jax.random.fold_in(key, 59)
    starts = jax.random.randint(key, (REQ, 1), 0, PROMPT_PAGES - MAXP + 1)
    return (starts + jnp.arange(MAXP, dtype=jnp.int32)[None, :]).astype(jnp.int32)


def draw_lengths(key, part):
    key = jax.random.fold_in(key, 71)
    span_key, pick_key = jax.random.split(key)
    spans = jax.random.randint(span_key, (REQ,), PAGE, MAXP * PAGE + 1)
    longest = jax.random.randint(pick_key, (), 0, REQ)
    return jnp.where(jnp.arange(REQ) == longest, MAXP * PAGE, spans).astype(jnp.int32)


def setup_inputs(seed: int = 0) -> dict:
    splits = jax.random.split(jax.random.key(seed), 8)
    return {
        "prefill_latent": draw_prefill_latent(jax.random.fold_in(splits[7], 71), 0),
        "stretch_page": draw_stretch_page(jax.random.fold_in(splits[7], 71), 0),
        "page_table": draw_page_table(jax.random.fold_in(splits[7], 71), 0),
        "page_list": draw_page_list(jax.random.fold_in(splits[7], 71), 0),
        "lengths": draw_lengths(jax.random.fold_in(splits[7], 71), 0),
        "queries": draw_queries(jax.random.fold_in(splits[7], 71), 0),
        "new_latent": draw_new_latent(jax.random.fold_in(splits[7], 71), 0),
    }


SOFTMAX_SCALE = 192.0 ** -0.5
MASKED_SCORE = -1e30


def reference(prefill_latent, stretch_page, page_table, page_list, lengths, queries, new_latent):
    logical = jnp.zeros_like(prefill_latent).at[stretch_page].set(prefill_latent)
    flat_slot = (page_table[:, 0] * SLOTS + page_table[:, 1]).astype(jnp.int32)
    cache_pool = jnp.zeros_like(prefill_latent).at[flat_slot].set(logical)
    position = jnp.arange(MAXP, dtype=jnp.int32)
    token_index = jnp.arange(PAGE, dtype=jnp.int32)
    order_index = jnp.arange(STEPS * ROWS, dtype=jnp.int32)
    visible = (order_index[None, :] <= order_index[:, None]).reshape(STEPS, ROWS, 1, STEPS * ROWS)

    def one_request(request_args):
        page_ids, length, query_rows, fresh_rows = request_args
        page_keys = cache_pool[flat_slot[page_ids]].astype(jnp.float32).reshape(CAPR, N_PAGES, PAGE, LATW)
        is_live = ((position[:, None] * PAGE + token_index[None, :]) < length).reshape(CAPR, N_PAGES, PAGE)
        query_wide = query_rows.astype(jnp.float32)
        scores = jnp.einsum("srhc,iqtc->srhiqt", query_wide, page_keys) * SOFTMAX_SCALE
        group_peak = jnp.max(jnp.where(is_live, scores, MASKED_SCORE), axis=(3, 5))
        group_weight = jnp.where(is_live, jnp.exp(scores - group_peak[:, :, :, None, :, None]), 0.0)
        group_total = jnp.sum(group_weight, axis=(3, 5))
        weights16 = lax.optimization_barrier(group_weight.astype(jnp.bfloat16))
        group_sum = jnp.einsum("srhiqt,iqtc->srhqc", weights16.astype(jnp.float32), page_keys[..., :LAT])
        fresh_wide = fresh_rows.astype(jnp.float32).reshape(STEPS * ROWS, LATW)
        fresh_scores = jnp.einsum("srhc,mc->srhm", query_wide, fresh_wide) * SOFTMAX_SCALE
        fresh_peak = jnp.max(jnp.where(visible, fresh_scores, MASKED_SCORE), axis=-1)
        fresh_weight = jnp.where(visible, jnp.exp(fresh_scores - fresh_peak[..., None]), 0.0)
        fresh_total = jnp.sum(fresh_weight, axis=-1)
        fresh16 = lax.optimization_barrier(fresh_weight.astype(jnp.bfloat16))
        fresh_sum = jnp.einsum("srhm,mc->srhc", fresh16.astype(jnp.float32), fresh_wide[:, :LAT])
        top_score = jnp.maximum(jnp.max(group_peak, axis=-1), fresh_peak)
        group_scale = jnp.exp(group_peak - top_score[..., None])
        fresh_scale = jnp.exp(fresh_peak - top_score)
        numerator = jnp.einsum("srhq,srhqc->srhc", group_scale, group_sum) + fresh_scale[..., None] * fresh_sum
        denominator = jnp.sum(group_scale * group_total, axis=-1) + fresh_scale * fresh_total
        return (numerator / denominator[..., None]).astype(jnp.bfloat16)

    attended = lax.map(one_request, (page_list, lengths, jnp.transpose(queries, (1, 0, 2, 3, 4)), jnp.transpose(new_latent, (1, 0, 2, 3))))
    return (jnp.transpose(attended, (1, 0, 2, 3, 4)), cache_pool)
```

```python
import functools

import jax
import jax.numpy as jnp
from jax import lax
from jax.experimental import pallas as pl
from jax.experimental.pallas import tpu as pltpu
from jax.sharding import PartitionSpec as P

LAT = 512
LATW = 576
WIDE = 640
PAGE = 64
NY = 8
NQ = 8
NZ = 8
SHARE = 8
SOFTMAX_SCALE = 192.0 ** (-0.5)
MASKED_SCORE = -1e30
F32 = jnp.float32
BF16 = jnp.bfloat16
I32 = jnp.int32


def iota(shape, dim):
    return lax.broadcasted_iota(I32, shape, dim)


def dot(a, b):
    return jnp.dot(a, b, preferred_element_type=F32)


def dot_last(a, b):
    return lax.dot_general(a, b, (((1,), (1,)), ((), ())), preferred_element_type=F32)


def kernel(
    prefill, stretch, table, plist, lengths, queries, fresh,
    out, cache,
    pages, sorted_pages, row_pages, gathered, picked, keys, all_queries,
    sums, sums_in, stats, stats_in,
    load_sem, s1_send, s1_recv, right_send, right_recv, left_send, left_recv,
    s3_send, s3_recv, q_send, q_recv, s4_send, s4_recv, st_send, st_recv,
):
    p = lax.axis_index("pages")
    z = lax.axis_index("heads")
    y = p // NQ
    q = lax.rem(p, NQ)

    def in_row(i):
        return (y * NQ + i, z)

    def in_column(i):
        return (i * NQ + q, z)

    def in_depth(i):
        return (p, i)

    right, left = lax.rem(y + 1, NY), lax.rem(y + NY - 1, NY)
    row_peers = [lax.rem(q + o, NQ) for o in range(1, NQ)]
    depth_peers = [lax.rem(z + o, NZ) for o in range(1, NZ)]

    barrier = pltpu.get_barrier_semaphore()
    targets = [in_row(i) for i in row_peers] + [in_column(right), in_column(left)]
    targets += [in_depth(i) for i in depth_peers]
    for target in targets:
        pl.semaphore_signal(barrier, inc=1, device_id=target, device_id_type=pl.DeviceIdType.MESH)

    load = pltpu.make_async_copy(
        prefill.at[:, pl.ds(pl.multiple_of((z // 2) * 16, 16), 16), :], pages, load_sem
    )
    load.start()

    def remote(src, dst, send, recv, target):
        return pltpu.make_async_remote_copy(
            src_ref=src, dst_ref=dst, send_sem=send, recv_sem=recv,
            device_id=target, device_id_type=pl.DeviceIdType.MESH,
        )

    shift = table[0:1, 0:1]
    own_queries = queries[...].reshape(64, LATW)
    all_queries[z] = own_queries

    load.wait()
    lane = iota((1, 128), 1)
    page_of_lane = jnp.zeros((1, 128), I32)
    for k in range(8):
        page_of_lane = jnp.where(lane // 16 == k, stretch[p * 8 + k], page_of_lane)
    residue = (page_of_lane + shift) & 7
    row = iota((64, 128), 0)
    col = iota((64, 128), 1)
    chosen = jnp.logical_and(residue == row // 8, (col & 15) == (row & 7) + 8 * lax.rem(z, 2))
    page_col = jnp.sum(jnp.where(chosen, page_of_lane, 0).astype(F32), axis=1, keepdims=True)
    page_int = page_col.astype(I32)
    ordered = dot(chosen.astype(F32).astype(BF16), pages[...].reshape(128, LATW))
    sorted_pages[:, :, 0:LATW] = ordered.reshape(8, 8, LATW)
    tail = iota((64, 64), 1)
    marks = jnp.where(tail < 32, page_int // 8, page_int & 7).astype(F32)
    sorted_pages[:, :, LATW:WIDE] = marks.reshape(8, 8, WIDE - LATW)

    pl.semaphore_wait(barrier, len(targets))

    s1 = []
    for n, i in enumerate(row_peers):
        copy = remote(sorted_pages.at[i], row_pages.at[q], s1_send.at[n], s1_recv.at[n], in_row(i))
        copy.start()
        s1.append(copy)
    qc = []
    for n, i in enumerate(depth_peers):
        copy = remote(all_queries.at[z], all_queries.at[z], q_send.at[n], q_recv.at[n], in_depth(i))
        copy.start()
        qc.append(copy)
    row_pages[q] = sorted_pages[q]
    for copy in s1:
        copy.wait_recv()
    gathered[y] = row_pages[...].reshape(64, WIDE).astype(BF16)

    ring = []
    for step in range(4):
        if step:
            ring[-2].wait_recv()
            ring[-1].wait_recv()
        give_right = lax.rem(y + NY - step, NY)
        give_left = lax.rem(y + step, NY)
        rows_right = pl.ds(0, 64 if step < 3 else 32)
        rows_left = pl.ds(0, 64) if step < 3 else pl.ds(32, 32)
        view = gathered.at[give_right, rows_right, :]
        copy = remote(view, view, right_send.at[step], right_recv.at[step], in_column(right))
        copy.start()
        ring.append(copy)
        view = gathered.at[give_left, rows_left, :]
        copy = remote(view, view, left_send.at[step], left_recv.at[step], in_column(left))
        copy.start()
        ring.append(copy)
    ring[-2].wait_recv()
    ring[-1].wait_recv()

    have = gathered[...].reshape(512, WIDE)
    mark_lane = iota((64, WIDE), 1)
    weigh = jnp.where(mark_lane == LATW, 64.0, jnp.where(mark_lane == LATW + 32, 8.0, 0.0))
    have_key = dot_last(weigh.astype(BF16), have) + (iota((64, 512), 1) & 7).astype(F32)
    have_key = have_key.astype(I32)
    for half in range(2):
        first = jnp.zeros((256, 1), I32)
        dest = iota((256, 1), 0) // 64
        for i in range(4):
            first = jnp.where(dest == i, plist[y * NQ + half * 4 + i, 0], first)
        first = first + ((q - shift - first) & 7)
        inner = iota((256, 1), 0) & 63
        want = (first + 8 * (inner // 8)) * 8 + (inner & 7)
        key = jnp.concatenate([have_key] * 4, axis=0)
        pick = (want == key).astype(F32).astype(BF16)
        picked[pl.ds(half * 4, 4)] = dot(pick, have).astype(BF16).reshape(4, 64, WIDE)
    s3 = []
    for n, i in enumerate(row_peers):
        copy = remote(picked.at[i], keys.at[q], s3_send.at[n], s3_recv.at[n], in_row(i))
        copy.start()
        s3.append(copy)
    keys[q] = picked[q]

    page = iota((512, 64), 0)
    slot = iota((512, 64), 1) // 8
    here = jnp.logical_and(table[:, 0:1] == p, table[:, 1:2] == slot)
    number = jnp.where(iota((512, 128), 1) < 64, iota((512, 128), 0) // 8, iota((512, 128), 0) & 7)
    lookup = lax.dot_general(
        here.astype(F32).astype(BF16), number.astype(F32).astype(BF16),
        (((0,), (0,)), ((), ())), preferred_element_type=F32,
    )
    want = (lookup[:, 0:1] * 64.0 + lookup[:, 64:65] * 8.0).astype(I32) + (iota((64, 1), 0) & 7)
    pick = (want == have_key).astype(F32).astype(BF16)
    cache[...] = dot(pick, have)[:, 0:LATW].reshape(8, 8, LATW).astype(BF16)

    fresh_rows = jnp.zeros((16, LATW), F32)
    fresh_index = iota((16, LATW), 0)
    for m in range(4):
        one = fresh[m // 2, 0, m % 2 : m % 2 + 1, :].astype(F32)
        fresh_rows = jnp.where(fresh_index == m, one, fresh_rows)
    fresh_rows = fresh_rows.astype(BF16)
    fresh_scores = dot_last(own_queries, fresh_rows) * SOFTMAX_SCALE
    seen = iota((64, 16), 1) <= iota((64, 16), 0) // 16
    fresh_peak = jnp.max(jnp.where(seen, fresh_scores, MASKED_SCORE), axis=1, keepdims=True)
    fresh_weight = jnp.where(seen, jnp.exp(fresh_scores - fresh_peak), 0.0)
    fresh_total = jnp.sum(fresh_weight, axis=1, keepdims=True)
    fresh_sum = dot(fresh_weight.astype(BF16), fresh_rows[:, 0:LAT])

    begin = plist[p, 0]
    token = iota((1, 512), 1)
    position = ((token // 64 - shift - begin) & 7) + 8 * ((token & 63) // 8)
    live = position * PAGE + z * SHARE + (token & 7) < lengths[p]

    for copy in qc:
        copy.wait_recv()
    for copy in s3:
        copy.wait_recv()
    latents = keys[...].reshape(512, WIDE)
    narrow = latents[:, 0:LATW]
    values = latents[:, 0:LAT]

    s4 = []
    stat_lane = iota((64, 128), 1)
    for n in range(NZ):
        i = lax.rem(z + n + 1, NZ)
        scores = dot_last(all_queries[i], narrow) * SOFTMAX_SCALE
        scores = jnp.where(live, scores, MASKED_SCORE)
        peak = jnp.max(scores, axis=1, keepdims=True)
        weight = jnp.where(live, jnp.exp(scores - peak), 0.0)
        total = jnp.sum(weight, axis=1, keepdims=True)
        summed = dot(weight.astype(BF16), values)
        stat = jnp.where(stat_lane == 0, peak, jnp.where(stat_lane == 1, total, 0.0))
        stat = jnp.transpose(stat)[0:8, :]
        if n < NZ - 1:
            sums[i] = summed.astype(BF16)
            stats[i, :, 0:64] = stat
            stats[i, :, 64:128] = stat
            copy = remote(stats.at[i], stats_in.at[z], st_send.at[n], st_recv.at[n], in_depth(i))
            copy.start()
            s4.append(copy)
            copy = remote(sums.at[i], sums_in.at[z], s4_send.at[n], s4_recv.at[n], in_depth(i))
            copy.start()
            s4.append(copy)
        else:
            stats_in[z, :, 0:64] = stat
            stats_in[z, :, 64:128] = stat
            own_sum = summed
            own_peak = peak

    for copy in s4:
        copy.wait_recv()
    peaks = stats_in[:, 0, :]
    totals = stats_in[:, 1, :]
    shared_peak = jnp.max(peaks, axis=0, keepdims=True)
    spread = jnp.concatenate(
        [peaks, totals, jnp.broadcast_to(shared_peak, (8, 128)), jnp.zeros((104, 128), F32)], axis=0
    )
    spread = jnp.transpose(spread)[0:64, :]
    top = jnp.maximum(spread[:, 16:17], fresh_peak)
    fresh_scale = jnp.exp(fresh_peak - top)
    numerator = fresh_scale * fresh_sum + jnp.exp(own_peak - top) * own_sum
    denominator = fresh_scale * fresh_total
    for n in range(NZ):
        scale = jnp.exp(spread[:, n : n + 1] - top)
        denominator = denominator + scale * spread[:, 8 + n : 9 + n]
    sums_in[z] = jnp.zeros((64, LAT), BF16)
    for n in range(NZ):
        scale = jnp.exp(spread[:, n : n + 1] - top)
        numerator = numerator + scale * sums_in[n].astype(F32)
    out[...] = (numerator / denominator).astype(BF16).reshape(2, 1, 2, 16, LAT)

    for copy in s1 + qc + ring + s3 + s4:
        copy.wait_send()


def local(prefill_latent, stretch_page, page_table, page_list, lengths, queries, new_latent):
    vmem = pl.BlockSpec(memory_space=pltpu.VMEM)
    smem = pl.BlockSpec(memory_space=pltpu.SMEM)
    dma = pltpu.SemaphoreType.DMA
    return pl.pallas_call(
        kernel,
        out_shape=(
            jax.ShapeDtypeStruct((2, 1, 2, 16, LAT), BF16),
            jax.ShapeDtypeStruct((8, 8, LATW), BF16),
        ),
        in_specs=[pl.BlockSpec(memory_space=pl.ANY), smem, vmem, smem, smem, vmem, vmem],
        out_specs=(vmem, vmem),
        scratch_shapes=[
            pltpu.VMEM((8, 16, LATW), BF16),
            pltpu.VMEM((8, 8, WIDE), F32),
            pltpu.VMEM((8, 8, WIDE), F32),
            pltpu.VMEM((8, 64, WIDE), BF16),
            pltpu.VMEM((8, 64, WIDE), BF16),
            pltpu.VMEM((8, 64, WIDE), BF16),
            pltpu.VMEM((8, 64, LATW), BF16),
            pltpu.VMEM((8, 64, LAT), BF16),
            pltpu.VMEM((8, 64, LAT), BF16),
            pltpu.VMEM((8, 8, 128), F32),
            pltpu.VMEM((8, 8, 128), F32),
            dma, dma((7,)), dma((7,)), dma((4,)), dma((4,)), dma((4,)), dma((4,)),
            dma((7,)), dma((7,)), dma((7,)), dma((7,)), dma((7,)), dma((7,)), dma((7,)), dma((7,)),
        ],
        compiler_params=pltpu.CompilerParams(
            collective_id=0, has_side_effects=True, vmem_limit_bytes=40 * 1024 * 1024
        ),
        name="place_and_attend",
    )(prefill_latent, stretch_page, page_table, page_list, lengths, queries, new_latent)


def solution(mesh):
    in_specs = (
        P("pages", None, None),
        P(),
        P(),
        P(),
        P(),
        P(None, "pages", None, "heads", None),
        P(None, "pages", None, None),
    )
    out_specs = (P(None, "pages", None, "heads", None), P("pages", "heads", None))
    return jax.shard_map(local, mesh=mesh, in_specs=in_specs, out_specs=out_specs, check_vma=False)
```

```python
import jax
import jax.numpy as jnp
from jax import lax
from jax.experimental import pallas as pl
from jax.experimental.pallas import tpu as pltpu
from jax.sharding import PartitionSpec as P

LAT = 512
LATW = 576
PAGE = 64
NY = 8
NQ = 8
NZ = 8
SHARE = 8
STARTS = (0, 256, 512)
WIDTHS = (256, 256, 128)
USED = (256, 256, 64)
SOFTMAX_SCALE = 192.0 ** (-0.5)
MASKED_SCORE = -1e30
F32 = jnp.float32
BF16 = jnp.bfloat16
I32 = jnp.int32
DEPTH_ORDER = (4, 3, 5, 2, 6, 1, 7)


def iota(shape, dim):
    return lax.broadcasted_iota(I32, shape, dim)


def dot(a, b):
    return jnp.dot(a, b, preferred_element_type=F32)


def dot_last(a, b):
    return lax.dot_general(a, b, (((1,), (1,)), ((), ())), preferred_element_type=F32)


def hot(mask):
    return mask.astype(F32).astype(BF16)


def kernel(
    prefill_hbm, stretch_hbm, stretch_row_hbm, table_hbm, plist_hbm, lengths_hbm, queries_hbm, fresh_hbm,
    out, cache,
    pages, stretch, stretch_row, table, plist, lengths, fresh,
    outgoing, incoming, all_queries, picks,
    gathered0, gathered1, gathered2, picked0, picked1, picked2, keys0, keys1, keys2,
    sums, sums_in, stats, stats_in,
    load_sem, s1_send, s1_recv, s2_send, s2_recv,
    s3_send, s3_recv, q_send, q_recv, s4_send, s4_recv, st_send, st_recv,
):
    gathered = (gathered0, gathered1, gathered2)
    picked = (picked0, picked1, picked2)
    keys = (keys0, keys1, keys2)
    p = lax.axis_index("pages")
    z = lax.axis_index("heads")
    y = p // NQ
    q = lax.rem(p, NQ)
    core = lax.rem(q, 2)

    def in_row(i):
        return (y * NQ + i, z)

    def in_column(step):
        return (lax.rem(y + NY + step, NY) * NQ + q, z)

    def in_depth(i):
        return (p, i)

    loads = []
    sources = (
        (prefill_hbm.at[:, pl.ds(pl.multiple_of((z // 2) * 16, 16), 16), :], pages),
        (stretch_hbm, stretch),
        (table_hbm, table),
        (queries_hbm.at[:, 0], all_queries.at[z]),
        (stretch_row_hbm, stretch_row),
        (plist_hbm.at[pl.ds(pl.multiple_of(y * NQ, NQ), NQ), :], plist),
        (lengths_hbm, lengths),
        (fresh_hbm, fresh),
    )
    for n, (src, dst) in enumerate(sources):
        copy = pltpu.make_async_copy(src, dst, load_sem.at[n])
        copy.start()
        loads.append(copy)

    barrier = pltpu.get_barrier_semaphore()
    row_peers = [lax.rem(q + o, NQ) for o in range(1, NQ)]
    depth_peers = [lax.rem(z + o, NZ) for o in DEPTH_ORDER]
    targets = [in_row(i) for i in row_peers] + [in_column(d) for d in (1, -1, 2, -2)]
    targets += [in_depth(i) for i in depth_peers]
    for target in targets:
        pl.semaphore_signal(barrier, inc=1, device_id=target, device_id_type=pl.DeviceIdType.MESH)

    def remote(src, dst, send, recv, target):
        return pltpu.make_async_remote_copy(
            src_ref=src, dst_ref=dst, send_sem=send, recv_sem=recv,
            device_id=target, device_id_type=pl.DeviceIdType.MESH,
        )

    for copy in loads[0:3]:
        copy.wait()
    shift = table[0:1, 0:1]
    lane = iota((1, 128), 1)
    page_of_lane = jnp.zeros((1, 128), I32)
    for k in range(8):
        page_of_lane = jnp.where(lane // 16 == k, stretch[p * 8 + k], page_of_lane)
    residue = (page_of_lane + shift) & 7
    row = iota((128, 128), 0)
    col = iota((128, 128), 1)
    chosen = jnp.logical_and(residue == row // 16, (col & 15) == (row & 7) + 8 * lax.rem(z, 2))
    ordered = dot(hot(chosen), pages[...].reshape(128, LATW)).astype(BF16).astype(F32)
    second = (iota((128, 256), 0) & 8) == 8
    body = jnp.where(second, ordered[:, 256:512], ordered[:, 0:256]).astype(BF16)
    outgoing[:, :, 0:256] = body.reshape(8, 16, 256)
    outgoing[:, :, 256:320] = ordered[:, 512:576].astype(BF16).reshape(8, 16, 64)
    outgoing[:, :, 320:384] = jnp.zeros((8, 16, 64), BF16)

    pl.semaphore_wait(barrier, len(targets))

    s1 = []
    for n, i in enumerate(row_peers):
        copy = remote(outgoing.at[i], incoming.at[q], s1_send.at[n], s1_recv.at[n], in_row(i))
        copy.start()
        s1.append(copy)
    incoming[q] = outgoing[q]

    for copy in loads[3:]:
        copy.wait()
    qc = []
    for n, i in enumerate(depth_peers):
        copy = remote(all_queries.at[z], all_queries.at[z], q_send.at[n], q_recv.at[n], in_depth(i))
        copy.start()
        qc.append(copy)
    numbers = stretch_row[...]
    mine = ((numbers + shift) & 7) == q
    parts = jnp.where(iota((8, 512), 0) == 0, numbers // 8, numbers & 7)
    parts = jnp.where(mine, parts, 0).astype(F32).astype(BF16)
    same = hot(iota((512, 512), 0) // 8 == iota((512, 512), 1) // 8)
    found = dot(parts, same)
    have_key = (found[0:1, :] * 64.0 + found[1:2, :] * 8.0).astype(I32) + (iota((1, 512), 1) & 7)
    for half in range(2):
        first = jnp.zeros((256, 1), I32)
        dest = iota((256, 1), 0) // 64
        for i in range(4):
            first = jnp.where(dest == i, plist[half * 4 + i, 0], first)
        first = first + ((q - shift - first) & 7)
        inner = iota((256, 1), 0) & 63
        want = (first + 8 * (inner // 8)) * 8 + (inner & 7)
        picks[pl.ds(half * 256, 256), :] = hot(want == have_key)

    for copy in s1:
        copy.wait_recv()
    arrived = incoming[...].astype(F32)
    gathered0[y] = arrived[:, 0:8, 0:256].reshape(64, 256).astype(BF16)
    gathered1[y] = arrived[:, 8:16, 0:256].reshape(64, 256).astype(BF16)
    gathered2[y] = arrived[:, 0:8, 256:384].reshape(64, 128).astype(BF16)

    s2 = []

    def along(c, kind, block, rows, step):
        view = gathered[c].at[lax.rem(block + NY, NY), pl.ds(rows[0], rows[1]), :]
        copy = remote(view, view, s2_send.at[c, kind], s2_recv.at[c, kind], in_column(step))
        copy.start()
        s2.append(copy)
        return copy

    near = []
    for c in range(3):
        near.append([
            along(c, 0, y, (0, 64), 2),
            along(c, 1, y, (0, 64), -2),
            along(c, 2, y, (0, 64), 1),
            along(c, 3, y, (0, 64), -1),
        ])
    far = []
    for c in range(3):
        near[c][0].wait_recv()
        below = [along(c, 4, y - 2, (0, 64), 1), along(c, 6, y - 2, (0, 32), 2)]
        near[c][1].wait_recv()
        far.append(below + [along(c, 5, y + 2, (0, 64), -1), along(c, 7, y + 2, (32, 32), -2)])

    own_queries = all_queries[z].reshape(64, LATW)
    fresh_rows = jnp.zeros((16, LATW), F32)
    fresh_index = iota((16, LATW), 0)
    for m in range(4):
        one = fresh[m // 2, 0, m % 2 : m % 2 + 1, :].astype(F32)
        fresh_rows = jnp.where(fresh_index == m, one, fresh_rows)
    fresh_rows = fresh_rows.astype(BF16)
    fresh_scores = dot_last(own_queries, fresh_rows) * SOFTMAX_SCALE
    seen = iota((64, 16), 1) <= iota((64, 16), 0) // 16
    fresh_peak = jnp.max(jnp.where(seen, fresh_scores, MASKED_SCORE), axis=1, keepdims=True)
    fresh_weight = jnp.where(seen, jnp.exp(fresh_scores - fresh_peak), 0.0)
    fresh_total = jnp.sum(fresh_weight, axis=1, keepdims=True)
    fresh_sum = dot(fresh_weight.astype(BF16), fresh_rows[:, 0:LAT])

    s3 = []

    def hand(c, m, parity):
        i = lax.rem(q // 2 + m, 4) * 2 + parity
        copy = remote(
            picked[c].at[i], keys[c].at[q], s3_send.at[c, m * 2 + parity], s3_recv.at[c, m * 2 + core], in_row(i)
        )
        copy.start()
        s3.append(copy)

    def hand_sibling(c):
        i = q + 1 - 2 * core
        copy = remote(picked[c].at[i], keys[c].at[q], s3_send.at[c, 0], s3_recv.at[c, 0], in_row(i))
        copy.start()
        s3.append(copy)

    def hand_core(c, parity):
        for m in (2, 1, 3):
            hand(c, m, parity)

    for c in range(3):
        for copy in near[c][2:] + far[c]:
            copy.wait_recv()
        have = gathered[c][...].reshape(512, WIDTHS[c])
        picked[c][...] = dot(picks[...], have).astype(BF16).reshape(8, 64, WIDTHS[c])
        if c < 2:
            hand_core(c, 0)
        if c == 0:
            hand_core(c, 1)
        hand_sibling(c)
        keys[c][q] = picked[c][q]
    hand_core(2, 0)
    hand_core(1, 1)
    hand_core(2, 1)

    slot = iota((64, 512), 0) // 8
    here = jnp.logical_and(table[0:1, :] == p, table[1:2, :] == slot)
    number = jnp.where(here, iota((64, 512), 1), 0).astype(F32)
    want = jnp.sum(number, axis=1, keepdims=True).astype(I32) * 8 + (iota((64, 1), 0) & 7)
    pick = hot(want == have_key)
    for c in range(3):
        have = gathered[c][...].reshape(512, WIDTHS[c])[:, 0 : USED[c]]
        rows = dot(pick, have).reshape(8, 8, USED[c]).astype(BF16)
        cache[:, :, STARTS[c] : STARTS[c] + USED[c]] = rows

    begin = plist[q, 0]
    token = iota((1, 512), 1)
    position = ((token // 64 - shift - begin) & 7) + 8 * ((token & 63) // 8)
    live = position * PAGE + z * SHARE + (token & 7) < lengths[p]

    for copy in qc:
        copy.wait_recv()
    for c in range(3):
        for n in range(8):
            if n == 1:
                continue
            if n == 0:
                source = q + 1 - 2 * core
            else:
                source = lax.rem(q // 2 + 4 - n // 2, 4) * 2 + n % 2
            remote(
                picked[c].at[source], keys[c].at[source], s3_send.at[c, n], s3_recv.at[c, n], in_row(source)
            ).wait_recv()
    latents = [keys[c][...].reshape(512, WIDTHS[c])[:, 0 : USED[c]] for c in range(3)]

    s4 = []
    s4_stats = []
    stat_lane = iota((64, 128), 1)
    for n in range(NZ):
        i = depth_peers[n] if n < NZ - 1 else z
        asked = all_queries[i].reshape(64, LATW)
        scores = dot_last(asked[:, 0:256], latents[0]) + dot_last(asked[:, 256:512], latents[1])
        scores = (scores + dot_last(asked[:, 512:576], latents[2])) * SOFTMAX_SCALE
        scores = jnp.where(live, scores, MASKED_SCORE)
        peak = jnp.max(scores, axis=1, keepdims=True)
        weight = jnp.where(live, jnp.exp(scores - peak), 0.0)
        total = jnp.sum(weight, axis=1, keepdims=True)
        weight = weight.astype(BF16)
        stat = jnp.where(stat_lane == 0, peak, jnp.where(stat_lane == 1, total, 0.0))
        stat = jnp.transpose(stat)[0:8, :]
        if n < NZ - 1:
            stats[i, :, 0:64] = stat
            stats[i, :, 64:128] = stat
            copy = remote(stats.at[i], stats_in.at[z], st_send.at[n], st_recv.at[n], in_depth(i))
            copy.start()
            s4_stats.append(copy)
            sums[i, :, 0:256] = dot(weight, latents[0]).astype(BF16)
            sums[i, :, 256:512] = dot(weight, latents[1]).astype(BF16)
            copy = remote(sums.at[i], sums_in.at[z], s4_send.at[n], s4_recv.at[n], in_depth(i))
            copy.start()
            s4.append(copy)
        else:
            stats_in[z, :, 0:64] = stat
            stats_in[z, :, 64:128] = stat
            own_sum = jnp.concatenate([dot(weight, latents[0]), dot(weight, latents[1])], axis=1)
            own_peak = peak

    for copy in s4_stats:
        copy.wait_recv()
    peaks = stats_in[:, 0, :]
    totals = stats_in[:, 1, :]
    shared_peak = jnp.max(peaks, axis=0, keepdims=True)
    scales = jnp.exp(peaks - shared_peak)
    shared_total = jnp.sum(scales * totals, axis=0, keepdims=True)
    spread = jnp.concatenate(
        [scales, jnp.broadcast_to(shared_peak, (8, 128)), jnp.broadcast_to(shared_total, (8, 128)),
         jnp.zeros((104, 128), F32)], axis=0
    )
    spread = jnp.transpose(spread)[0:64, :]
    cached_peak = spread[:, 8:9]
    top = jnp.maximum(cached_peak, fresh_peak)
    fresh_scale = jnp.exp(fresh_peak - top)
    cached_scale = jnp.exp(cached_peak - top)
    denominator = fresh_scale * fresh_total + cached_scale * spread[:, 16:17]
    numerator = fresh_scale * fresh_sum + jnp.exp(own_peak - top) * own_sum
    spread_lane = iota((64, 128), 1)
    for n, o in enumerate(DEPTH_ORDER):
        source = lax.rem(z + NZ - o, NZ)
        s4[n].wait_recv()
        scale = jnp.sum(jnp.where(spread_lane == source, spread, 0.0), axis=1, keepdims=True) * cached_scale
        numerator = numerator + scale * sums_in[source].astype(F32)
    out[...] = (numerator / denominator).astype(BF16).reshape(2, 1, 2, 16, LAT)

    for copy in s1 + qc + s2 + s3 + s4_stats + s4:
        copy.wait_send()


def local(prefill_latent, stretch_page, page_table, page_list, lengths, queries, new_latent):
    vmem = pl.BlockSpec(memory_space=pltpu.VMEM)
    hbm = pl.BlockSpec(memory_space=pltpu.HBM)
    dma = pltpu.SemaphoreType.DMA
    blocks = [pltpu.VMEM((8, 64, width), BF16) for width in WIDTHS]
    return pl.pallas_call(
        kernel,
        out_shape=(
            jax.ShapeDtypeStruct((2, 1, 2, 16, LAT), BF16),
            jax.ShapeDtypeStruct((8, 8, LATW), BF16),
        ),
        in_specs=[hbm] * 8,
        out_specs=(vmem, vmem),
        scratch_shapes=[
            pltpu.VMEM((8, 16, LATW), BF16),
            pltpu.SMEM((512,), I32),
            pltpu.VMEM((1, 512), I32),
            pltpu.VMEM((2, 512), I32),
            pltpu.SMEM((8, 64), I32),
            pltpu.SMEM((64,), I32),
            pltpu.VMEM((2, 1, 2, LATW), BF16),
            pltpu.VMEM((8, 16, 384), BF16),
            pltpu.VMEM((8, 16, 384), BF16),
            pltpu.VMEM((8, 2, 2, 16, LATW), BF16),
            pltpu.VMEM((512, 512), BF16),
            *blocks, *blocks, *blocks,
            pltpu.VMEM((8, 64, LAT), BF16),
            pltpu.VMEM((8, 64, LAT), BF16),
            pltpu.VMEM((8, 8, 128), F32),
            pltpu.VMEM((8, 8, 128), F32),
            dma((8,)), dma((7,)), dma((7,)), dma((3, 8)), dma((3, 8)),
            dma((3, 8)), dma((3, 8)), dma((7,)), dma((7,)), dma((7,)), dma((7,)), dma((7,)), dma((7,)),
        ],
        compiler_params=pltpu.CompilerParams(
            collective_id=0, has_side_effects=True, vmem_limit_bytes=24 * 1024 * 1024
        ),
        name="place_and_attend",
    )(*[pltpu.with_memory_space_constraint(x, pltpu.HBM) for x in (
        prefill_latent, stretch_page, stretch_page.reshape(1, 512), page_table.T, page_list, lengths,
        queries, new_latent)]
    )


def solution(mesh):
    in_specs = (
        P("pages", None, None),
        P(),
        P(),
        P(),
        P(),
        P(None, "pages", None, "heads", None),
        P(None, "pages", None, None),
    )
    out_specs = (P(None, "pages", None, "heads", None), P("pages", "heads", None))
    return jax.shard_map(local, mesh=mesh, in_specs=in_specs, out_specs=out_specs, check_vma=False)
```

```python
import jax
import jax.numpy as jnp
from jax import lax
from jax.experimental import pallas as pl
from jax.experimental.pallas import tpu as pltpu
from jax.sharding import PartitionSpec as P

LAT = 512
LATW = 576
PAGE = 64
NY = 8
NQ = 8
NZ = 8
SHARE = 8
STARTS = (512, 0, 256)
WIDTHS = (128, 256, 256)
USED = (64, 256, 256)
SOFTMAX_SCALE = 192.0 ** (-0.5)
MASKED_SCORE = -1e30
F32 = jnp.float32
BF16 = jnp.bfloat16
I32 = jnp.int32
DEPTH_ORDER = (4, 3, 5, 2, 6, 1, 7)
BATCHES = ((3, 5, 4, 2), (6, 1, 7, 0))


def iota(shape, dim):
    return lax.broadcasted_iota(I32, shape, dim)


def dot(a, b):
    return jnp.dot(a, b, preferred_element_type=F32)


def dot_last(a, b):
    return lax.dot_general(a, b, (((1,), (1,)), ((), ())), preferred_element_type=F32)


def hot(mask):
    return mask.astype(F32).astype(BF16)


def kernel(
    prefill_hbm, stretch_hbm, stretch_row_hbm, table_hbm, plist_hbm, lengths_hbm, queries_hbm, fresh_hbm,
    out, cache,
    pages, stretch, stretch_row, table, plist, lengths, fresh,
    outgoing, incoming, all_queries, picks,
    gathered0, gathered1, gathered2, picked0, picked1, picked2, keys0, keys1, keys2,
    sums, sums_in, stats, stats_in,
    load_sem, s1_send, s1_recv, s2_send, s2_recv,
    s3_send, s3_recv, q_send, q_recv, s4_send, s4_recv,
):
    gathered = (gathered0, gathered1, gathered2)
    picked = (picked0, picked1, picked2)
    keys = (keys0, keys1, keys2)
    p = lax.axis_index("pages")
    z = lax.axis_index("heads")
    y = p // NQ
    q = lax.rem(p, NQ)
    core = lax.rem(q, 2)

    def in_row(i):
        return (y * NQ + i, z)

    def in_column(step):
        return (lax.rem(y + NY + step, NY) * NQ + q, z)

    def in_depth(i):
        return (p, i)

    loads = []
    sources = (
        (prefill_hbm.at[:, pl.ds(pl.multiple_of((z // 2) * 16, 16), 16), :], pages),
        (stretch_hbm, stretch),
        (table_hbm, table),
        (queries_hbm.at[:, 0], all_queries.at[z]),
        (stretch_row_hbm, stretch_row),
        (plist_hbm.at[pl.ds(pl.multiple_of(y * NQ, NQ), NQ), :], plist),
        (lengths_hbm, lengths),
        (fresh_hbm, fresh),
    )
    for n, (src, dst) in enumerate(sources):
        copy = pltpu.make_async_copy(src, dst, load_sem.at[n])
        copy.start()
        loads.append(copy)

    barrier = pltpu.get_barrier_semaphore()
    row_peers = [lax.rem(q + o, NQ) for o in range(1, NQ)]
    depth_peers = [lax.rem(z + o, NZ) for o in DEPTH_ORDER]
    targets = [in_row(i) for i in row_peers] + [in_column(d) for d in (1, -1, 2, -2)]
    targets += [in_depth(i) for i in depth_peers]
    for target in targets:
        pl.semaphore_signal(barrier, inc=1, device_id=target, device_id_type=pl.DeviceIdType.MESH)

    def remote(src, dst, send, recv, target):
        return pltpu.make_async_remote_copy(
            src_ref=src, dst_ref=dst, send_sem=send, recv_sem=recv,
            device_id=target, device_id_type=pl.DeviceIdType.MESH,
        )

    for copy in loads[0:3]:
        copy.wait()
    shift = table[0:1, 0:1]
    lane = iota((1, 128), 1)
    page_of_lane = jnp.zeros((1, 128), I32)
    for k in range(8):
        page_of_lane = jnp.where(lane // 16 == k, stretch[p * 8 + k], page_of_lane)
    residue = (page_of_lane + shift) & 7
    row = iota((128, 128), 0)
    col = iota((128, 128), 1)
    chosen = jnp.logical_and(residue == row // 16, (col & 15) == (row & 7) + 8 * lax.rem(z, 2))
    ordered = dot(hot(chosen), pages[...].reshape(128, LATW)).astype(BF16).astype(F32)
    second = (iota((128, 256), 0) & 8) == 8
    body = jnp.where(second, ordered[:, 256:512], ordered[:, 0:256]).astype(BF16)
    outgoing[:, :, 0:256] = body.reshape(8, 16, 256)
    outgoing[:, :, 256:320] = ordered[:, 512:576].astype(BF16).reshape(8, 16, 64)
    outgoing[:, :, 320:384] = jnp.zeros((8, 16, 64), BF16)

    pl.semaphore_wait(barrier, len(targets))

    s1 = []
    for n, i in enumerate(row_peers):
        copy = remote(outgoing.at[i], incoming.at[q], s1_send.at[n], s1_recv.at[n], in_row(i))
        copy.start()
        s1.append(copy)
    incoming[q] = outgoing[q]

    for copy in loads[3:]:
        copy.wait()
    qc = []
    for n, i in enumerate(depth_peers):
        copy = remote(all_queries.at[z], all_queries.at[z], q_send.at[n], q_recv.at[n], in_depth(i))
        copy.start()
        qc.append(copy)
    for copy in s1:
        copy.wait_recv()
    arrived = incoming[...].astype(F32)
    gathered0[y] = arrived[:, 0:8, 256:384].reshape(64, 128).astype(BF16)
    gathered1[y] = arrived[:, 0:8, 0:256].reshape(64, 256).astype(BF16)
    gathered2[y] = arrived[:, 8:16, 0:256].reshape(64, 256).astype(BF16)

    s2 = []

    def along(c, kind, block, rows, step):
        view = gathered[c].at[lax.rem(block + NY, NY), pl.ds(rows[0], rows[1]), :]
        copy = remote(view, view, s2_send.at[c, kind], s2_recv.at[c, kind], in_column(step))
        copy.start()
        s2.append(copy)
        return copy

    near = []
    far = []

    def start_near(c):
        near.append([
            along(c, 0, y, (0, 64), 2),
            along(c, 1, y, (0, 64), -2),
            along(c, 2, y, (0, 64), 1),
            along(c, 3, y, (0, 64), -1),
        ])

    def start_far(c):
        near[c][0].wait_recv()
        below = [along(c, 4, y - 2, (0, 64), 1), along(c, 6, y - 2, (0, 32), 2)]
        near[c][1].wait_recv()
        far.append(below + [along(c, 5, y + 2, (0, 64), -1), along(c, 7, y + 2, (32, 32), -2)])

    start_near(0)
    start_near(1)

    numbers = stretch_row[...]
    mine = ((numbers + shift) & 7) == q
    parts = jnp.where(iota((8, 512), 0) == 0, numbers // 8, numbers & 7)
    parts = jnp.where(mine, parts, 0).astype(F32).astype(BF16)
    same = hot(iota((512, 512), 0) // 8 == iota((512, 512), 1) // 8)
    found = dot(parts, same)
    have_key = (found[0:1, :] * 64.0 + found[1:2, :] * 8.0).astype(I32) + (iota((1, 512), 1) & 7)
    for half in range(2):
        first = jnp.zeros((256, 1), I32)
        dest = iota((256, 1), 0) // 64
        for i in range(4):
            first = jnp.where(dest == i, plist[half * 4 + i, 0], first)
        first = first + ((q - shift - first) & 7)
        inner = iota((256, 1), 0) & 63
        want = (first + 8 * (inner // 8)) * 8 + (inner & 7)
        picks[pl.ds(half * 256, 256), :] = hot(want == have_key)

    start_far(0)
    start_near(2)
    start_far(1)
    start_far(2)

    own_queries = all_queries[z].reshape(64, LATW)
    fresh_rows = jnp.zeros((16, LATW), F32)
    fresh_index = iota((16, LATW), 0)
    for m in range(4):
        one = fresh[m // 2, 0, m % 2 : m % 2 + 1, :].astype(F32)
        fresh_rows = jnp.where(fresh_index == m, one, fresh_rows)
    fresh_rows = fresh_rows.astype(BF16)
    fresh_scores = dot_last(own_queries, fresh_rows) * SOFTMAX_SCALE
    seen = iota((64, 16), 1) <= iota((64, 16), 0) // 16
    fresh_peak = jnp.max(jnp.where(seen, fresh_scores, MASKED_SCORE), axis=1, keepdims=True)
    fresh_weight = jnp.where(seen, jnp.exp(fresh_scores - fresh_peak), 0.0)
    fresh_total = jnp.sum(fresh_weight, axis=1, keepdims=True)
    fresh_sum = dot(fresh_weight.astype(BF16), fresh_rows[:, 0:LAT])

    s3 = []

    def hand(c, m, parity):
        i = lax.rem(q // 2 + m, 4) * 2 + parity
        copy = remote(
            picked[c].at[i], keys[c].at[q], s3_send.at[c, m * 2 + parity], s3_recv.at[c, m * 2 + core], in_row(i)
        )
        copy.start()
        s3.append(copy)

    def hand_sibling(c):
        i = q + 1 - 2 * core
        copy = remote(picked[c].at[i], keys[c].at[q], s3_send.at[c, 0], s3_recv.at[c, 0], in_row(i))
        copy.start()
        s3.append(copy)

    def hand_core(c, parity):
        for m in (2, 1, 3):
            hand(c, m, parity)

    for c in range(3):
        for copy in near[c][2:] + far[c]:
            copy.wait_recv()
        have = gathered[c][...].reshape(512, WIDTHS[c])
        picked[c][...] = dot(picks[...], have).astype(BF16).reshape(8, 64, WIDTHS[c])
        hand_core(c, 0)
        hand_core(c, 1)
        hand_sibling(c)
        keys[c][q] = picked[c][q]

    slot = iota((64, 512), 0) // 8
    here = jnp.logical_and(table[0:1, :] == p, table[1:2, :] == slot)
    number = jnp.where(here, iota((64, 512), 1), 0).astype(F32)
    want = jnp.sum(number, axis=1, keepdims=True).astype(I32) * 8 + (iota((64, 1), 0) & 7)
    pick = hot(want == have_key)
    for c in range(3):
        have = gathered[c][...].reshape(512, WIDTHS[c])[:, 0 : USED[c]]
        rows = dot(pick, have).reshape(8, 8, USED[c]).astype(BF16)
        cache[:, :, STARTS[c] : STARTS[c] + USED[c]] = rows

    begin = plist[q, 0]
    token = iota((1, 512), 1)
    position = ((token // 64 - shift - begin) & 7) + 8 * ((token & 63) // 8)
    live = position * PAGE + z * SHARE + (token & 7) < lengths[p]

    for copy in qc:
        copy.wait_recv()
    for c in range(3):
        for n in range(8):
            if n == 1:
                continue
            if n == 0:
                source = q + 1 - 2 * core
            else:
                source = lax.rem(q // 2 + 4 - n // 2, 4) * 2 + n % 2
            remote(
                picked[c].at[source], keys[c].at[source], s3_send.at[c, n], s3_recv.at[c, n], in_row(source)
            ).wait_recv()
    latents = [keys[c][...].reshape(512, WIDTHS[c])[:, 0 : USED[c]] for c in range(3)]

    s4 = []

    def send(n, src, dst, target):
        copy = remote(src, dst, s4_send.at[n], s4_recv.at[n], in_depth(target))
        copy.start()
        s4.append(copy)
        return copy

    def stat_block(peak, total):
        lane = iota((64, 128), 1)
        block = jnp.transpose(jnp.where(lane == 0, peak, jnp.where(lane == 1, total, 0.0)))[0:8, :]
        return jnp.concatenate([block, block], axis=1)

    def share(offsets):
        asked = jnp.concatenate([all_queries[depth[o]].reshape(64, LATW) for o in offsets], axis=0)
        scores = dot_last(asked[:, 0:256], latents[1]) + dot_last(asked[:, 256:512], latents[2])
        scores = (scores + dot_last(asked[:, 512:576], latents[0])) * SOFTMAX_SCALE
        scores = jnp.where(live, scores, MASKED_SCORE)
        peak = jnp.max(scores, axis=1, keepdims=True)
        weight = jnp.where(live, jnp.exp(scores - peak), 0.0)
        total = jnp.sum(weight, axis=1, keepdims=True)
        weight = weight.astype(BF16)
        summed = [dot(weight, latents[1]), dot(weight, latents[2])]
        terms = {}
        for k, o in enumerate(offsets):
            rows = slice(64 * k, 64 * k + 64)
            terms[o] = (jnp.concatenate([part[rows] for part in summed], axis=1), peak[rows], total[rows])
        return terms

    depth = [lax.rem(z + o, NZ) for o in range(NZ)]
    arrivals = {}
    terms = share(BATCHES[0])
    for o in (3, 5, 4):
        summed, peak, total = terms[o]
        sums[o] = summed.astype(BF16)
        stats[o] = stat_block(peak, total)
    arrivals["stat3"] = send(0, stats.at[3], stats_in.at[0], depth[1])
    arrivals["stat5"] = send(1, stats.at[5], stats_in.at[1], depth[7])
    arrivals["stat4"] = send(2, stats.at[4], stats_in.at[2], depth[2])
    arrivals["stat4b"] = send(3, stats.at[4], stats_in.at[3], depth[6])
    arrivals["sum3"] = send(4, sums.at[3], sums_in.at[0], depth[1])
    arrivals["sum5"] = send(5, sums.at[5], sums_in.at[1], depth[7])
    arrivals["sum4"] = send(6, sums.at[4, pl.ds(0, 32), :], sums_in.at[2, pl.ds(0, 32), :], depth[2])
    arrivals["sum4b"] = send(7, sums.at[4, pl.ds(32, 32), :], sums_in.at[2, pl.ds(32, 32), :], depth[6])
    ahead = terms[2]
    terms = share(BATCHES[1])
    behind = terms[6]
    for o in (1, 7):
        summed, peak, total = terms[o]
        sums[o] = summed.astype(BF16)
        stats[o] = stat_block(peak, total)
    arrivals["stat1"] = send(8, stats.at[1], stats_in.at[4], depth[1])
    arrivals["stat7"] = send(9, stats.at[7], stats_in.at[5], depth[7])
    arrivals["sum1"] = send(10, sums.at[1], sums_in.at[3], depth[1])
    arrivals["sum7"] = send(11, sums.at[7], sums_in.at[4], depth[7])
    own_sum, own_peak, own_total = terms[0]

    def columns(blocks):
        filled = jnp.concatenate(blocks + [jnp.zeros((128 - 8 * len(blocks), 128), F32)], axis=0)
        return jnp.transpose(filled)[0:64, :]

    def relay(own, full, half, first_rows):
        own_sum, own_peak, own_total = own
        arrivals["stat3" if first_rows else "stat5"].wait_recv()
        arrivals["stat4" if first_rows else "stat4b"].wait_recv()
        spread = columns([stats_in[full], stats_in[half]])
        inside = iota((64, 1), 0) < 32
        if not first_rows:
            inside = jnp.logical_not(inside)
        full_peak = spread[:, 0:1]
        half_peak = jnp.where(inside, spread[:, 8:9], MASKED_SCORE)
        half_total = jnp.where(inside, spread[:, 9:10], 0.0)
        peak = jnp.maximum(jnp.maximum(own_peak, full_peak), half_peak)
        own_scale = jnp.exp(own_peak - peak)
        full_scale = jnp.exp(full_peak - peak)
        half_scale = jnp.exp(half_peak - peak)
        total = own_scale * own_total + full_scale * spread[:, 1:2] + half_scale * half_total
        arrivals["sum3" if first_rows else "sum5"].wait_recv()
        merged = own_scale * own_sum + full_scale * sums_in[full].astype(F32)
        arrivals["sum4" if first_rows else "sum4b"].wait_recv()
        rows = slice(0, 32) if first_rows else slice(32, 64)
        extra = half_scale[rows] * sums_in[2, rows, :].astype(F32)
        pieces = [merged[0:32], merged[32:64]]
        pieces[0 if first_rows else 1] = pieces[0 if first_rows else 1] + extra
        return jnp.concatenate(pieces, axis=0), peak, total

    for n, (own, full, half, first_rows) in enumerate(((ahead, 0, 2, True), (behind, 1, 3, False))):
        summed, peak, total = relay(own, full, half, first_rows)
        o = 2 if first_rows else 6
        stats[o] = stat_block(peak, total)
        arrivals["stat%d" % o] = send(12 + n, stats.at[o], stats_in.at[6 + n], depth[o])
        sums[o] = summed.astype(BF16)
        arrivals["sum%d" % o] = send(14 + n, sums.at[o], sums_in.at[5 + n], depth[o])

    for name in ("stat1", "stat7", "stat2", "stat6"):
        arrivals[name].wait_recv()
    spread = columns([stats_in[k] for k in (4, 5, 6, 7)])
    peaks = [spread[:, 8 * k : 8 * k + 1] for k in range(4)]
    totals = [spread[:, 8 * k + 1 : 8 * k + 2] for k in range(4)]
    top = jnp.maximum(own_peak, fresh_peak)
    for peak in peaks:
        top = jnp.maximum(top, peak)
    fresh_scale = jnp.exp(fresh_peak - top)
    own_scale = jnp.exp(own_peak - top)
    scales = [jnp.exp(peak - top) for peak in peaks]
    denominator = fresh_scale * fresh_total + own_scale * own_total
    for scale, total in zip(scales, totals):
        denominator = denominator + scale * total
    numerator = fresh_scale * fresh_sum + own_scale * own_sum
    for k, name in enumerate(("sum1", "sum7", "sum2", "sum6")):
        arrivals[name].wait_recv()
        numerator = numerator + scales[k] * sums_in[3 + k].astype(F32)
    out[...] = (numerator / denominator).astype(BF16).reshape(2, 1, 2, 16, LAT)

    for copy in s1 + qc + s2 + s3 + s4:
        copy.wait_send()


def local(prefill_latent, stretch_page, page_table, page_list, lengths, queries, new_latent):
    vmem = pl.BlockSpec(memory_space=pltpu.VMEM)
    hbm = pl.BlockSpec(memory_space=pltpu.HBM)
    dma = pltpu.SemaphoreType.DMA
    blocks = [pltpu.VMEM((8, 64, width), BF16) for width in WIDTHS]
    return pl.pallas_call(
        kernel,
        out_shape=(
            jax.ShapeDtypeStruct((2, 1, 2, 16, LAT), BF16),
            jax.ShapeDtypeStruct((8, 8, LATW), BF16),
        ),
        in_specs=[hbm] * 8,
        out_specs=(vmem, vmem),
        scratch_shapes=[
            pltpu.VMEM((8, 16, LATW), BF16),
            pltpu.SMEM((512,), I32),
            pltpu.VMEM((1, 512), I32),
            pltpu.VMEM((2, 512), I32),
            pltpu.SMEM((8, 64), I32),
            pltpu.SMEM((64,), I32),
            pltpu.VMEM((2, 1, 2, LATW), BF16),
            pltpu.VMEM((8, 16, 384), BF16),
            pltpu.VMEM((8, 16, 384), BF16),
            pltpu.VMEM((8, 2, 2, 16, LATW), BF16),
            pltpu.VMEM((512, 512), BF16),
            *blocks, *blocks, *blocks,
            pltpu.VMEM((8, 64, LAT), BF16),
            pltpu.VMEM((8, 64, LAT), BF16),
            pltpu.VMEM((8, 8, 128), F32),
            pltpu.VMEM((8, 8, 128), F32),
            dma((8,)), dma((7,)), dma((7,)), dma((3, 8)), dma((3, 8)),
            dma((3, 8)), dma((3, 8)), dma((7,)), dma((7,)), dma((16,)), dma((16,)),
        ],
        compiler_params=pltpu.CompilerParams(
            collective_id=0, has_side_effects=True, vmem_limit_bytes=24 * 1024 * 1024
        ),
        name="place_and_attend",
    )(*[pltpu.with_memory_space_constraint(x, pltpu.HBM) for x in (
        prefill_latent, stretch_page, stretch_page.reshape(1, 512), page_table.T, page_list, lengths,
        queries, new_latent)]
    )


def solution(mesh):
    in_specs = (
        P("pages", None, None),
        P(),
        P(),
        P(),
        P(),
        P(None, "pages", None, "heads", None),
        P(None, "pages", None, None),
    )
    out_specs = (P(None, "pages", None, "heads", None), P("pages", "heads", None))
    return jax.shard_map(local, mesh=mesh, in_specs=in_specs, out_specs=out_specs, check_vma=False)
```

```python
import jax
import jax.numpy as jnp
from jax import lax
from jax.experimental import pallas as pl
from jax.experimental.pallas import tpu as pltpu
from jax.sharding import PartitionSpec as P

LAT = 512
LATW = 576
PAGE = 64
NY = 8
NQ = 8
NZ = 8
SHARE = 8
WIDE = 640
CHUNKS = ((512, 128), (0, 256), (256, 256))
SOFTMAX_SCALE = 192.0 ** (-0.5)
MASKED_SCORE = -1e30
F32 = jnp.float32
BF16 = jnp.bfloat16
I32 = jnp.int32
FIRST = 2
ORDER = (
    ("near", 0),
    ("near", 1),
    ("far", 0),
    ("near", 2),
    ("far", 1),
    ("pass", 0),
    ("far", 2),
    ("pass", 1),
    ("pass", 2),
)
HALVES = (pl.ds(0, 256), pl.ds(256, 256))
DEPTH_ORDER = (4, 3, 5, 2, 6, 1, 7)
BATCHES = ((3, 5, 4, 2), (6, 1, 7, 0))


def iota(shape, dim):
    return lax.broadcasted_iota(I32, shape, dim)


def dot(a, b):
    return jnp.dot(a, b, preferred_element_type=F32)


def dot_last(a, b):
    return lax.dot_general(a, b, (((1,), (1,)), ((), ())), preferred_element_type=F32)


def hot(mask):
    return mask.astype(F32).astype(BF16)


def kernel(
    prefill_hbm, stretch_hbm, stretch_row_hbm, table_hbm, plist_hbm, lengths_hbm, queries_hbm, fresh_hbm,
    out, cache,
    pages, stretch, stretch_row, table, plist, lengths, fresh,
    outgoing, incoming, all_queries, picks,
    sums, sums_in, stats, stats_in,
    load_sem, s1_send, s1_recv, s2_send, s2_recv,
    s3_send, s3_recv, q_send, q_recv, s4_send, s4_recv, *blocks,
):
    chunks = len(CHUNKS)
    gathered, picked, keys = blocks[:chunks], blocks[chunks : 2 * chunks], blocks[2 * chunks :]
    p = lax.axis_index("pages")
    z = lax.axis_index("heads")
    y = p // NQ
    q = lax.rem(p, NQ)
    core = lax.rem(q, 2)

    def in_row(i):
        return (y * NQ + i, z)

    def in_column(step):
        return (lax.rem(y + NY + step, NY) * NQ + q, z)

    def in_depth(i):
        return (p, i)

    loads = []
    sources = (
        (prefill_hbm.at[:, pl.ds(pl.multiple_of((z // 2) * 16, 16), 16), :], pages),
        (stretch_hbm, stretch),
        (table_hbm, table),
        (queries_hbm.at[:, 0], all_queries.at[z]),
        (stretch_row_hbm, stretch_row),
        (plist_hbm.at[pl.ds(pl.multiple_of(y * NQ, NQ), NQ), :], plist),
        (lengths_hbm, lengths),
        (fresh_hbm, fresh),
    )
    for n, (src, dst) in enumerate(sources):
        copy = pltpu.make_async_copy(src, dst, load_sem.at[n])
        copy.start()
        loads.append(copy)

    barrier = pltpu.get_barrier_semaphore()
    row_peers = [lax.rem(q + o, NQ) for o in range(1, NQ)]
    depth_peers = [lax.rem(z + o, NZ) for o in DEPTH_ORDER]
    targets = [in_row(i) for i in row_peers] + [in_column(d) for d in (1, -1, 2, -2)]
    targets += [in_depth(i) for i in depth_peers]
    for target in targets:
        pl.semaphore_signal(barrier, inc=1, device_id=target, device_id_type=pl.DeviceIdType.MESH)

    def remote(src, dst, send, recv, target):
        return pltpu.make_async_remote_copy(
            src_ref=src, dst_ref=dst, send_sem=send, recv_sem=recv,
            device_id=target, device_id_type=pl.DeviceIdType.MESH,
        )

    for copy in loads[0:3]:
        copy.wait()
    shift = table[0:1, 0:1]
    lane = iota((1, 128), 1)
    page_of_lane = jnp.zeros((1, 128), I32)
    for k in range(8):
        page_of_lane = jnp.where(lane // 16 == k, stretch[p * 8 + k], page_of_lane)
    residue = (page_of_lane + shift) & 7
    row = iota((128, 128), 0)
    col = iota((128, 128), 1)
    chosen = jnp.logical_and(residue == row // 16, (col & 15) == (row & 7) + 8 * lax.rem(z, 2))
    ordered = dot(hot(chosen), pages[...].reshape(128, LATW)).astype(BF16).astype(F32)
    second = (iota((128, 256), 0) & 8) == 8
    body = jnp.where(second, ordered[:, 256:512], ordered[:, 0:256]).astype(BF16)
    outgoing[:, :, 0:256] = body.reshape(8, 16, 256)
    outgoing[:, :, 256:320] = ordered[:, 512:576].astype(BF16).reshape(8, 16, 64)
    outgoing[:, :, 320:384] = jnp.zeros((8, 16, 64), BF16)

    pl.semaphore_wait(barrier, len(targets))

    s1 = []
    for n, i in enumerate(row_peers):
        copy = remote(outgoing.at[i], incoming.at[q], s1_send.at[n], s1_recv.at[n], in_row(i))
        copy.start()
        s1.append(copy)
    incoming[q] = outgoing[q]

    for copy in loads[3:]:
        copy.wait()
    qc = []
    for n, i in enumerate(depth_peers):
        copy = remote(all_queries.at[z], all_queries.at[z], q_send.at[n], q_recv.at[n], in_depth(i))
        copy.start()
        qc.append(copy)
    for copy in s1:
        copy.wait_recv()
    arrived = incoming[...].astype(F32)
    whole = jnp.concatenate([arrived[:, 0:8, 0:256], arrived[:, 8:16, 0:256], arrived[:, 0:8, 256:384]], axis=2)
    whole = whole.reshape(64, WIDE).astype(BF16)
    for c, (start, width) in enumerate(CHUNKS):
        gathered[c][y] = whole[:, start : start + width]

    s2 = []

    def along(c, kind, block, rows, step):
        view = gathered[c].at[lax.rem(block + NY, NY), pl.ds(rows[0], rows[1]), :]
        copy = remote(view, view, s2_send.at[c, kind], s2_recv.at[c, kind], in_column(step))
        copy.start()
        s2.append(copy)
        return copy

    near = []
    far = []

    def start_near(c):
        near.append([
            along(c, 0, y, (0, 64), 2),
            along(c, 1, y, (0, 64), -2),
            along(c, 2, y, (0, 64), 1),
            along(c, 3, y, (0, 64), -1),
        ])

    def start_far(c):
        near[c][0].wait_recv()
        below = [along(c, 4, y - 2, (0, 64), 1), along(c, 6, y - 2, (0, 32), 2)]
        near[c][1].wait_recv()
        far.append(below + [along(c, 5, y + 2, (0, 64), -1), along(c, 7, y + 2, (32, 32), -2)])

    s3 = []

    def part(ref, i, c):
        return ref[c].at[i]

    def hand(c, m, parity):
        i = lax.rem(q // 2 + m, 4) * 2 + parity
        copy = remote(
            part(picked, i, c), part(keys, q, c), s3_send.at[c, m * 2 + parity], s3_recv.at[c, m * 2 + core], in_row(i)
        )
        copy.start()
        s3.append(copy)

    def hand_sibling(c):
        i = q + 1 - 2 * core
        copy = remote(part(picked, i, c), part(keys, q, c), s3_send.at[c, 0], s3_recv.at[c, 0], in_row(i))
        copy.start()
        s3.append(copy)

    def hand_core(c, parity):
        for m in (2, 1, 3):
            hand(c, m, parity)

    def pass_on(c):
        for copy in near[c][2:] + far[c]:
            copy.wait_recv()
        width = CHUNKS[c][1]
        have = gathered[c][...].reshape(512, width)
        picked[c][...] = dot(picks[...], have).astype(BF16).reshape(8, 64, width)
        hand_core(c, 0)
        hand_core(c, 1)
        hand_sibling(c)
        keys[c][q] = picked[c][q]

    start = {"near": start_near, "far": start_far, "pass": pass_on}
    for kind, c in ORDER[:FIRST]:
        start[kind](c)

    numbers = stretch_row[...]
    mine = ((numbers + shift) & 7) == q
    parts = jnp.where(iota((8, 512), 0) == 0, numbers // 8, numbers & 7)
    parts = jnp.where(mine, parts, 0).astype(F32).astype(BF16)
    same = hot(iota((512, 512), 0) // 8 == iota((512, 512), 1) // 8)
    found = dot(parts, same)
    have_key = (found[0:1, :] * 64.0 + found[1:2, :] * 8.0).astype(I32) + (iota((1, 512), 1) & 7)
    for half in range(2):
        first = jnp.zeros((256, 1), I32)
        dest = iota((256, 1), 0) // 64
        for i in range(4):
            first = jnp.where(dest == i, plist[half * 4 + i, 0], first)
        first = first + ((q - shift - first) & 7)
        inner = iota((256, 1), 0) & 63
        want = (first + 8 * (inner // 8)) * 8 + (inner & 7)
        picks[pl.ds(half * 256, 256), :] = hot(want == have_key)

    for kind, c in ORDER[FIRST:]:
        start[kind](c)

    own_queries = all_queries[z].reshape(64, LATW)
    fresh_rows = jnp.zeros((16, LATW), F32)
    fresh_index = iota((16, LATW), 0)
    for m in range(4):
        one = fresh[m // 2, 0, m % 2 : m % 2 + 1, :].astype(F32)
        fresh_rows = jnp.where(fresh_index == m, one, fresh_rows)
    fresh_rows = fresh_rows.astype(BF16)
    fresh_scores = dot_last(own_queries, fresh_rows) * SOFTMAX_SCALE
    seen = iota((64, 16), 1) <= iota((64, 16), 0) // 16
    fresh_peak = jnp.max(jnp.where(seen, fresh_scores, MASKED_SCORE), axis=1, keepdims=True)
    fresh_weight = jnp.where(seen, jnp.exp(fresh_scores - fresh_peak), 0.0)
    fresh_total = jnp.sum(fresh_weight, axis=1, keepdims=True)
    fresh_sum = dot(fresh_weight.astype(BF16), fresh_rows[:, 0:LAT])

    def joined(refs):
        order = sorted(range(chunks), key=lambda c: CHUNKS[c][0])
        return jnp.concatenate([refs[c][...].reshape(512, CHUNKS[c][1]) for c in order], axis=1)

    slot = iota((64, 512), 0) // 8
    here = jnp.logical_and(table[0:1, :] == p, table[1:2, :] == slot)
    number = jnp.where(here, iota((64, 512), 1), 0).astype(F32)
    want = jnp.sum(number, axis=1, keepdims=True).astype(I32) * 8 + (iota((64, 1), 0) & 7)
    pick = hot(want == have_key)
    cache[...] = dot(pick, joined(gathered)[:, 0:LATW]).reshape(8, 8, LATW).astype(BF16)

    begin = plist[q, 0]
    token = iota((1, 512), 1)
    position = ((token // 64 - shift - begin) & 7) + 8 * ((token & 63) // 8)
    live = position * PAGE + z * SHARE + (token & 7) < lengths[p]

    for copy in qc:
        copy.wait_recv()
    for c in range(len(CHUNKS)):
        for n in range(8):
            if n == 1:
                continue
            if n == 0:
                source = q + 1 - 2 * core
            else:
                source = lax.rem(q // 2 + 4 - n // 2, 4) * 2 + n % 2
            remote(
                part(picked, source, c), part(keys, source, c), s3_send.at[c, n], s3_recv.at[c, n], in_row(source)
            ).wait_recv()
    latents = joined(keys)
    narrow = latents[:, 0:LATW]
    values = latents[:, 0:LAT]

    s4 = []

    def send(n, src, dst, target):
        copy = remote(src, dst, s4_send.at[n], s4_recv.at[n], in_depth(target))
        copy.start()
        s4.append(copy)
        return copy

    def stat_block(peak, total):
        lane = iota((64, 128), 1)
        block = jnp.transpose(jnp.where(lane == 0, peak, jnp.where(lane == 1, total, 0.0)))[0:8, :]
        return jnp.concatenate([block, block], axis=1)

    def share(offsets):
        asked = jnp.concatenate([all_queries[depth[o]].reshape(64, LATW) for o in offsets], axis=0)
        scores = dot_last(asked, narrow) * SOFTMAX_SCALE
        scores = jnp.where(live, scores, MASKED_SCORE)
        peak = jnp.max(scores, axis=1, keepdims=True)
        weight = jnp.where(live, jnp.exp(scores - peak), 0.0)
        total = jnp.sum(weight, axis=1, keepdims=True)
        weight = weight.astype(BF16)
        summed = dot(weight, values)
        terms = {}
        for k, o in enumerate(offsets):
            rows = slice(64 * k, 64 * k + 64)
            terms[o] = (summed[rows], peak[rows], total[rows])
        return terms

    depth = [lax.rem(z + o, NZ) for o in range(NZ)]
    arrivals = {}
    terms = share(BATCHES[0])
    for o in (3, 5, 4):
        summed, peak, total = terms[o]
        sums[o] = summed.astype(BF16)
        stats[o] = stat_block(peak, total)
    arrivals["stat3"] = send(0, stats.at[3], stats_in.at[0], depth[1])
    arrivals["stat5"] = send(1, stats.at[5], stats_in.at[1], depth[7])
    arrivals["stat4"] = send(2, stats.at[4], stats_in.at[2], depth[2])
    arrivals["stat4b"] = send(3, stats.at[4], stats_in.at[3], depth[6])
    for h, lanes in enumerate(HALVES):
        arrivals["sum3", h] = send(8 + h, sums.at[3, :, lanes], sums_in.at[0, :, lanes], depth[1])
        arrivals["sum5", h] = send(12 + h, sums.at[5, :, lanes], sums_in.at[1, :, lanes], depth[7])
        top_rows, low_rows = pl.ds(0, 32), pl.ds(32, 32)
        arrivals["sum4", h] = send(16 + h, sums.at[4, top_rows, lanes], sums_in.at[2, top_rows, lanes], depth[2])
        arrivals["sum4b", h] = send(20 + h, sums.at[4, low_rows, lanes], sums_in.at[2, low_rows, lanes], depth[6])
    ahead = terms[2]
    terms = share(BATCHES[1])
    behind = terms[6]
    for o in (1, 7):
        summed, peak, total = terms[o]
        sums[o] = summed.astype(BF16)
        stats[o] = stat_block(peak, total)
    arrivals["stat1"] = send(4, stats.at[1], stats_in.at[4], depth[1])
    arrivals["stat7"] = send(5, stats.at[7], stats_in.at[5], depth[7])
    arrivals["sum1"] = send(32, sums.at[1], sums_in.at[3], depth[1])
    arrivals["sum7"] = send(33, sums.at[7], sums_in.at[4], depth[7])
    own_sum, own_peak, own_total = terms[0]

    def columns(blocks):
        filled = jnp.concatenate(blocks + [jnp.zeros((128 - 8 * len(blocks), 128), F32)], axis=0)
        return jnp.transpose(filled)[0:64, :]

    def relay_scales(own, full, half, first_rows):
        _, own_peak, own_total = own
        arrivals["stat3" if first_rows else "stat5"].wait_recv()
        arrivals["stat4" if first_rows else "stat4b"].wait_recv()
        spread = columns([stats_in[full], stats_in[half]])
        inside = iota((64, 1), 0) < 32
        if not first_rows:
            inside = jnp.logical_not(inside)
        full_peak = spread[:, 0:1]
        half_peak = jnp.where(inside, spread[:, 8:9], MASKED_SCORE)
        half_total = jnp.where(inside, spread[:, 9:10], 0.0)
        peak = jnp.maximum(jnp.maximum(own_peak, full_peak), half_peak)
        own_scale = jnp.exp(own_peak - peak)
        full_scale = jnp.exp(full_peak - peak)
        half_scale = jnp.exp(half_peak - peak)
        total = own_scale * own_total + full_scale * spread[:, 1:2] + half_scale * half_total
        return peak, total, own_scale, full_scale, half_scale

    routes = ((ahead, 0, 2, True), (behind, 1, 3, False))
    route_scales = []
    for n, route in enumerate(routes):
        peak, total, *rest = relay_scales(*route)
        route_scales.append(rest)
        o = 2 if route[3] else 6
        stats[o] = stat_block(peak, total)
        arrivals["stat%d" % o] = send(6 + n, stats.at[o], stats_in.at[6 + n], depth[o])
    for h, lanes in enumerate(HALVES):
        cut = slice(lanes.start, lanes.start + lanes.size)
        for n, (own, full, half, first_rows) in enumerate(routes):
            own_scale, full_scale, half_scale = route_scales[n]
            arrivals["sum3" if first_rows else "sum5", h].wait_recv()
            merged = own_scale * own[0][:, cut] + full_scale * sums_in[full, :, cut].astype(F32)
            arrivals["sum4" if first_rows else "sum4b", h].wait_recv()
            rows = slice(0, 32) if first_rows else slice(32, 64)
            extra = half_scale[rows] * sums_in[2, rows, cut].astype(F32)
            pieces = [merged[0:32], merged[32:64]]
            k = 0 if first_rows else 1
            pieces[k] = pieces[k] + extra
            o = 2 if first_rows else 6
            sums[o, :, cut] = jnp.concatenate(pieces, axis=0).astype(BF16)
            arrivals["sum%d" % o, h] = send(24 + 4 * n + h, sums.at[o, :, lanes], sums_in.at[5 + n, :, lanes], depth[o])

    for name in ("stat1", "stat7", "stat2", "stat6"):
        arrivals[name].wait_recv()
    spread = columns([stats_in[k] for k in (4, 5, 6, 7)])
    peaks = [spread[:, 8 * k : 8 * k + 1] for k in range(4)]
    totals = [spread[:, 8 * k + 1 : 8 * k + 2] for k in range(4)]
    top = jnp.maximum(own_peak, fresh_peak)
    for peak in peaks:
        top = jnp.maximum(top, peak)
    fresh_scale = jnp.exp(fresh_peak - top)
    own_scale = jnp.exp(own_peak - top)
    scales = [jnp.exp(peak - top) for peak in peaks]
    denominator = fresh_scale * fresh_total + own_scale * own_total
    for scale, total in zip(scales, totals):
        denominator = denominator + scale * total
    numerator = fresh_scale * fresh_sum + own_scale * own_sum
    for k, name in enumerate(("sum1", "sum7")):
        arrivals[name].wait_recv()
        numerator = numerator + scales[k] * sums_in[3 + k].astype(F32)
    inverse = 1.0 / denominator
    for h, lanes in enumerate(HALVES):
        cut = slice(lanes.start, lanes.start + lanes.size)
        piece = numerator[:, cut]
        for n, name in enumerate(("sum2", "sum6")):
            arrivals[name, h].wait_recv()
            piece = piece + scales[2 + n] * sums_in[5 + n, :, cut].astype(F32)
        out[:, :, :, :, cut] = (piece * inverse).astype(BF16).reshape(2, 1, 2, 16, lanes.size)

    for copy in s1 + qc + s2 + s3 + s4:
        copy.wait_send()


def local(prefill_latent, stretch_page, page_table, page_list, lengths, queries, new_latent):
    vmem = pl.BlockSpec(memory_space=pltpu.VMEM)
    hbm = pl.BlockSpec(memory_space=pltpu.HBM)
    dma = pltpu.SemaphoreType.DMA
    chunks = len(CHUNKS)
    blocks = [pltpu.VMEM((8, 64, width), BF16) for _, width in CHUNKS]
    return pl.pallas_call(
        kernel,
        out_shape=(
            jax.ShapeDtypeStruct((2, 1, 2, 16, LAT), BF16),
            jax.ShapeDtypeStruct((8, 8, LATW), BF16),
        ),
        in_specs=[hbm] * 8,
        out_specs=(vmem, vmem),
        scratch_shapes=[
            pltpu.VMEM((8, 16, LATW), BF16),
            pltpu.SMEM((512,), I32),
            pltpu.VMEM((1, 512), I32),
            pltpu.VMEM((2, 512), I32),
            pltpu.SMEM((8, 64), I32),
            pltpu.SMEM((64,), I32),
            pltpu.VMEM((2, 1, 2, LATW), BF16),
            pltpu.VMEM((8, 16, 384), BF16),
            pltpu.VMEM((8, 16, 384), BF16),
            pltpu.VMEM((8, 2, 2, 16, LATW), BF16),
            pltpu.VMEM((512, 512), BF16),
            pltpu.VMEM((8, 64, LAT), BF16),
            pltpu.VMEM((8, 64, LAT), BF16),
            pltpu.VMEM((8, 8, 128), F32),
            pltpu.VMEM((8, 8, 128), F32),
            dma((8,)), dma((7,)), dma((7,)), dma((chunks, 8)), dma((chunks, 8)),
            dma((chunks, 8)), dma((chunks, 8)), dma((7,)), dma((7,)), dma((34,)), dma((34,)),
            *blocks, *blocks, *blocks,
        ],
        compiler_params=pltpu.CompilerParams(
            collective_id=0, has_side_effects=True, vmem_limit_bytes=24 * 1024 * 1024
        ),
        name="place_and_attend",
    )(*[pltpu.with_memory_space_constraint(x, pltpu.HBM) for x in (
        prefill_latent, stretch_page, stretch_page.reshape(1, 512), page_table.T, page_list, lengths,
        queries, new_latent)]
    )


def solution(mesh):
    in_specs = (
        P("pages", None, None),
        P(),
        P(),
        P(),
        P(),
        P(None, "pages", None, "heads", None),
        P(None, "pages", None, None),
    )
    out_specs = (P(None, "pages", None, "heads", None), P("pages", "heads", None))
    return jax.shard_map(local, mesh=mesh, in_specs=in_specs, out_specs=out_specs, check_vma=False)
```

```python
import jax
import jax.numpy as jnp
from jax import lax
from jax.experimental import pallas as pl
from jax.experimental.pallas import tpu as pltpu
from jax.sharding import PartitionSpec as P

LAT = 512
LATW = 576
PAGE = 64
NY = 8
NQ = 8
NZ = 8
SHARE = 8
WIDE = 640
CHUNKS = ((512, 128), (0, 256), (256, 256))
SOFTMAX_SCALE = 192.0 ** (-0.5)
MASKED_SCORE = -1e30
F32 = jnp.float32
BF16 = jnp.bfloat16
I32 = jnp.int32
FIRST = 2
ORDER = (
    ("near", 0),
    ("near", 1),
    ("far", 0),
    ("near", 2),
    ("far", 1),
    ("pass", 0),
    ("far", 2),
    ("pass", 1),
    ("pass", 2),
)
HALVES = (pl.ds(0, 256), pl.ds(256, 256))
DEPTH_ORDER = (4, 3, 5, 2, 6, 1, 7)
BATCHES = ((3, 5, 4, 2), (6, 1, 7, 0))


def iota(shape, dim):
    return lax.broadcasted_iota(I32, shape, dim)


def dot(a, b):
    return jnp.dot(a, b, preferred_element_type=F32)


def dot_last(a, b):
    return lax.dot_general(a, b, (((1,), (1,)), ((), ())), preferred_element_type=F32)


def hot(mask):
    return mask.astype(F32).astype(BF16)


def kernel(
    prefill_hbm, stretch_hbm, stretch_row_hbm, table_hbm, plist_hbm, lengths_hbm, queries_hbm, fresh_hbm,
    out, cache,
    pages, stretch, stretch_row, table, plist, lengths, fresh,
    outgoing, incoming, all_queries, picks,
    sums, sums_in, stats, stats_in,
    load_sem, s1_send, s1_recv, s2_send, s2_recv,
    s3_send, s3_recv, q_send, q_recv, s4_send, s4_recv, st_send, *blocks,
):
    chunks = len(CHUNKS)
    gathered, picked, keys = blocks[:chunks], blocks[chunks : 2 * chunks], blocks[2 * chunks :]
    p = lax.axis_index("pages")
    z = lax.axis_index("heads")
    y = p // NQ
    q = lax.rem(p, NQ)
    core = lax.rem(q, 2)

    def in_row(i):
        return (y * NQ + i, z)

    def in_column(step):
        return (lax.rem(y + NY + step, NY) * NQ + q, z)

    def in_depth(i):
        return (p, i)

    loads = []
    sources = (
        (prefill_hbm.at[:, pl.ds(pl.multiple_of((z // 2) * 16, 16), 16), :], pages),
        (stretch_hbm, stretch),
        (table_hbm, table),
        (queries_hbm.at[:, 0], all_queries.at[z]),
        (stretch_row_hbm, stretch_row),
        (plist_hbm.at[pl.ds(pl.multiple_of(y * NQ, NQ), NQ), :], plist),
        (lengths_hbm, lengths),
        (fresh_hbm, fresh),
    )
    for n, (src, dst) in enumerate(sources):
        copy = pltpu.make_async_copy(src, dst, load_sem.at[n])
        copy.start()
        loads.append(copy)

    barrier = pltpu.get_barrier_semaphore()
    row_peers = [lax.rem(q + o, NQ) for o in range(1, NQ)]
    depth_peers = [lax.rem(z + o, NZ) for o in DEPTH_ORDER]
    targets = [in_row(i) for i in row_peers] + [in_column(d) for d in (1, -1, 2, -2)]
    targets += [in_depth(i) for i in depth_peers]
    for target in targets:
        pl.semaphore_signal(barrier, inc=1, device_id=target, device_id_type=pl.DeviceIdType.MESH)

    def drain(ref, sem):
        pltpu.make_async_copy(ref, ref, sem).wait()

    def remote(src, dst, send, recv, target):
        return pltpu.make_async_remote_copy(
            src_ref=src, dst_ref=dst, send_sem=send, recv_sem=recv,
            device_id=target, device_id_type=pl.DeviceIdType.MESH,
        )

    for copy in loads[0:3]:
        copy.wait()
    shift = table[0:1, 0:1]
    lane = iota((1, 128), 1)
    page_of_lane = jnp.zeros((1, 128), I32)
    for k in range(8):
        page_of_lane = jnp.where(lane // 16 == k, stretch[p * 8 + k], page_of_lane)
    residue = (page_of_lane + shift) & 7
    row = iota((128, 128), 0)
    col = iota((128, 128), 1)
    chosen = jnp.logical_and(residue == row // 16, (col & 15) == (row & 7) + 8 * lax.rem(z, 2))
    ordered = dot(hot(chosen), pages[...].reshape(128, LATW)).astype(BF16).astype(F32)
    second = (iota((128, 256), 0) & 8) == 8
    body = jnp.where(second, ordered[:, 256:512], ordered[:, 0:256]).astype(BF16)
    outgoing[:, :, 0:256] = body.reshape(8, 16, 256)
    outgoing[:, :, 256:320] = ordered[:, 512:576].astype(BF16).reshape(8, 16, 64)
    outgoing[:, :, 320:384] = jnp.zeros((8, 16, 64), BF16)

    pl.semaphore_wait(barrier, len(targets))

    for i in row_peers:
        copy = remote(outgoing.at[i], incoming.at[q], s1_send, s1_recv, in_row(i))
        copy.start()
    incoming[q] = outgoing[q]

    for copy in loads[3:]:
        copy.wait()
    for i in depth_peers:
        remote(all_queries.at[z], all_queries.at[z], q_send, q_recv, in_depth(i)).start()
    drain(incoming.at[pl.ds(0, 7)], s1_recv)
    arrived = incoming[...].astype(F32)
    whole = jnp.concatenate([arrived[:, 0:8, 0:256], arrived[:, 8:16, 0:256], arrived[:, 0:8, 256:384]], axis=2)
    whole = whole.reshape(64, WIDE).astype(BF16)
    for c, (start, width) in enumerate(CHUNKS):
        gathered[c][y] = whole[:, start : start + width]


    def along(c, kind, block, rows, step):
        view = gathered[c].at[lax.rem(block + NY, NY), pl.ds(rows[0], rows[1]), :]
        remote(view, view, s2_send.at[c], s2_recv.at[c, min(kind, 2)], in_column(step)).start()

    def start_near(c):
        along(c, 0, y, (0, 64), 2)
        along(c, 1, y, (0, 64), -2)
        along(c, 2, y, (0, 64), 1)
        along(c, 3, y, (0, 64), -1)

    def start_far(c):
        drain(gathered[c].at[0], s2_recv.at[c, 0])
        along(c, 4, y - 2, (0, 64), 1)
        along(c, 6, y - 2, (0, 32), 2)
        drain(gathered[c].at[0], s2_recv.at[c, 1])
        along(c, 5, y + 2, (0, 64), -1)
        along(c, 7, y + 2, (32, 32), -2)

    def part(ref, i, c):
        return ref[c].at[i]

    def hand(c, m, parity):
        i = lax.rem(q // 2 + m, 4) * 2 + parity
        copy = remote(
            part(picked, i, c), part(keys, q, c), s3_send.at[c], s3_recv.at[c], in_row(i)
        )
        copy.start()

    def hand_sibling(c):
        i = q + 1 - 2 * core
        copy = remote(part(picked, i, c), part(keys, q, c), s3_send.at[c], s3_recv.at[c], in_row(i))
        copy.start()

    def hand_core(c, parity):
        for m in (2, 1, 3):
            hand(c, m, parity)

    def pass_on(c):
        drain(gathered[c].at[pl.ds(0, 5)], s2_recv.at[c, 2])
        width = CHUNKS[c][1]
        have = gathered[c][...].reshape(512, width)
        picked[c][...] = dot(picks[...], have).astype(BF16).reshape(8, 64, width)
        for m in (2, 1, 3):
            hand(c, m, 0)
            hand(c, m, 1)
        hand_sibling(c)
        keys[c][q] = picked[c][q]

    start = {"near": start_near, "far": start_far, "pass": pass_on}
    for kind, c in ORDER[:FIRST]:
        start[kind](c)

    numbers = stretch_row[...]
    mine = ((numbers + shift) & 7) == q
    parts = jnp.where(iota((8, 512), 0) == 0, numbers // 8, numbers & 7)
    parts = jnp.where(mine, parts, 0).astype(F32).astype(BF16)
    same = hot(iota((512, 512), 0) // 8 == iota((512, 512), 1) // 8)
    found = dot(parts, same)
    have_key = (found[0:1, :] * 64.0 + found[1:2, :] * 8.0).astype(I32) + (iota((1, 512), 1) & 7)
    for half in range(2):
        first = jnp.zeros((256, 1), I32)
        dest = iota((256, 1), 0) // 64
        for i in range(4):
            first = jnp.where(dest == i, plist[half * 4 + i, 0], first)
        first = first + ((q - shift - first) & 7)
        inner = iota((256, 1), 0) & 63
        want = (first + 8 * (inner // 8)) * 8 + (inner & 7)
        picks[pl.ds(half * 256, 256), :] = hot(want == have_key)

    for kind, c in ORDER[FIRST:]:
        start[kind](c)

    own_queries = all_queries[z].reshape(64, LATW)
    fresh_rows = jnp.zeros((16, LATW), F32)
    fresh_index = iota((16, LATW), 0)
    for m in range(4):
        one = fresh[m // 2, 0, m % 2 : m % 2 + 1, :].astype(F32)
        fresh_rows = jnp.where(fresh_index == m, one, fresh_rows)
    fresh_rows = fresh_rows.astype(BF16)
    fresh_scores = dot_last(own_queries, fresh_rows) * SOFTMAX_SCALE
    seen = iota((64, 16), 1) <= iota((64, 16), 0) // 16
    fresh_peak = jnp.max(jnp.where(seen, fresh_scores, MASKED_SCORE), axis=1, keepdims=True)
    fresh_weight = jnp.where(seen, jnp.exp(fresh_scores - fresh_peak), 0.0)
    fresh_total = jnp.sum(fresh_weight, axis=1, keepdims=True)
    fresh_sum = dot(fresh_weight.astype(BF16), fresh_rows[:, 0:LAT])

    def joined(refs):
        order = sorted(range(chunks), key=lambda c: CHUNKS[c][0])
        return jnp.concatenate([refs[c][...].reshape(512, CHUNKS[c][1]) for c in order], axis=1)

    slot = iota((64, 512), 0) // 8
    here = jnp.logical_and(table[0:1, :] == p, table[1:2, :] == slot)
    number = jnp.where(here, iota((64, 512), 1), 0).astype(F32)
    want = jnp.sum(number, axis=1, keepdims=True).astype(I32) * 8 + (iota((64, 1), 0) & 7)
    pick = hot(want == have_key)
    cache[...] = dot(pick, joined(gathered)[:, 0:LATW]).reshape(8, 8, LATW).astype(BF16)

    begin = plist[q, 0]
    token = iota((1, 512), 1)
    position = ((token // 64 - shift - begin) & 7) + 8 * ((token & 63) // 8)
    live = position * PAGE + z * SHARE + (token & 7) < lengths[p]

    drain(all_queries.at[pl.ds(0, 7)], q_recv)
    for c in range(chunks):
        drain(keys[c].at[pl.ds(0, 7)], s3_recv.at[c])
    latents = joined(keys)
    narrow = latents[:, 0:LATW]
    values = latents[:, 0:LAT]


    def send(src, dst, sem, target):
        remote(src, dst, s4_send, s4_recv.at[sem], in_depth(target)).start()

    def send_stat(src, dst, sem, target):
        remote(stats.at[src], stats_in.at[dst], st_send, s4_recv.at[sem], in_depth(target)).start()

    def stat_block(peak, total):
        lane = iota((64, 128), 1)
        block = jnp.transpose(jnp.where(lane == 0, peak, jnp.where(lane == 1, total, 0.0)))[0:8, :]
        return jnp.concatenate([block, block], axis=1)

    def share(offsets):
        asked = jnp.concatenate([all_queries[depth[o]].reshape(64, LATW) for o in offsets], axis=0)
        scores = dot_last(asked, narrow) * SOFTMAX_SCALE
        scores = jnp.where(live, scores, MASKED_SCORE)
        peak = jnp.max(scores, axis=1, keepdims=True)
        weight = jnp.where(live, jnp.exp(scores - peak), 0.0)
        total = jnp.sum(weight, axis=1, keepdims=True)
        weight = weight.astype(BF16)
        summed = dot(weight, values)
        terms = {}
        for k, o in enumerate(offsets):
            rows = slice(64 * k, 64 * k + 64)
            terms[o] = (summed[rows], peak[rows], total[rows])
        return terms

    depth = [lax.rem(z + o, NZ) for o in range(NZ)]
    terms = share(BATCHES[0])
    for o in (3, 5, 4):
        summed, peak, total = terms[o]
        sums[o] = summed.astype(BF16)
        stats[o] = stat_block(peak, total)
    send_stat(3, 0, 0, depth[1])
    send_stat(5, 1, 0, depth[7])
    send_stat(4, 2, 0, depth[2])
    send_stat(4, 3, 0, depth[6])
    top_rows, low_rows = pl.ds(0, 32), pl.ds(32, 32)
    for h, lanes in enumerate(HALVES):
        send(sums.at[3, :, lanes], sums_in.at[0, :, lanes], 2 + h, depth[1])
        send(sums.at[5, :, lanes], sums_in.at[1, :, lanes], 2 + h, depth[7])
        send(sums.at[4, top_rows, lanes], sums_in.at[2, top_rows, lanes], 2 + h, depth[2])
        send(sums.at[4, low_rows, lanes], sums_in.at[2, low_rows, lanes], 2 + h, depth[6])
    ahead = terms[2]
    terms = share(BATCHES[1])
    behind = terms[6]
    for o in (1, 7):
        summed, peak, total = terms[o]
        sums[o] = summed.astype(BF16)
        stats[o] = stat_block(peak, total)
    send_stat(1, 4, 1, depth[1])
    send_stat(7, 5, 1, depth[7])
    send(sums.at[1], sums_in.at[3], 4, depth[1])
    send(sums.at[7], sums_in.at[4], 4, depth[7])
    own_sum, own_peak, own_total = terms[0]

    def columns(blocks):
        filled = jnp.concatenate(blocks + [jnp.zeros((128 - 8 * len(blocks), 128), F32)], axis=0)
        return jnp.transpose(filled)[0:64, :]

    def relay_scales(own, full, half, first_rows):
        _, own_peak, own_total = own
        spread = columns([stats_in[full], stats_in[half]])
        inside = iota((64, 1), 0) < 32
        if not first_rows:
            inside = jnp.logical_not(inside)
        full_peak = spread[:, 0:1]
        half_peak = jnp.where(inside, spread[:, 8:9], MASKED_SCORE)
        half_total = jnp.where(inside, spread[:, 9:10], 0.0)
        peak = jnp.maximum(jnp.maximum(own_peak, full_peak), half_peak)
        own_scale = jnp.exp(own_peak - peak)
        full_scale = jnp.exp(full_peak - peak)
        half_scale = jnp.exp(half_peak - peak)
        total = own_scale * own_total + full_scale * spread[:, 1:2] + half_scale * half_total
        return peak, total, own_scale, full_scale, half_scale

    routes = ((ahead, 0, 2, True), (behind, 1, 3, False))
    route_scales = []
    drain(stats_in.at[pl.ds(0, 4)], s4_recv.at[0])
    for n, route in enumerate(routes):
        peak, total, *rest = relay_scales(*route)
        route_scales.append(rest)
        o = 2 if route[3] else 6
        stats[o] = stat_block(peak, total)
        send_stat(o, 6 + n, 1, depth[o])
    for h, lanes in enumerate(HALVES):
        cut = slice(lanes.start, lanes.start + lanes.size)
        drain(sums_in.at[pl.ds(0, 3), :, lanes], s4_recv.at[2 + h])
        for n, (own, full, half, first_rows) in enumerate(routes):
            own_scale, full_scale, half_scale = route_scales[n]
            merged = own_scale * own[0][:, cut] + full_scale * sums_in[full, :, cut].astype(F32)
            rows = slice(0, 32) if first_rows else slice(32, 64)
            extra = half_scale[rows] * sums_in[2, rows, cut].astype(F32)
            pieces = [merged[0:32], merged[32:64]]
            k = 0 if first_rows else 1
            pieces[k] = pieces[k] + extra
            o = 2 if first_rows else 6
            sums[o, :, cut] = jnp.concatenate(pieces, axis=0).astype(BF16)
            send(sums.at[o, :, lanes], sums_in.at[5 + n, :, lanes], 5 + h, depth[o])

    drain(stats_in.at[pl.ds(4, 4)], s4_recv.at[1])
    spread = columns([stats_in[k] for k in (4, 5, 6, 7)])
    peaks = [spread[:, 8 * k : 8 * k + 1] for k in range(4)]
    totals = [spread[:, 8 * k + 1 : 8 * k + 2] for k in range(4)]
    top = jnp.maximum(own_peak, fresh_peak)
    for peak in peaks:
        top = jnp.maximum(top, peak)
    fresh_scale = jnp.exp(fresh_peak - top)
    own_scale = jnp.exp(own_peak - top)
    scales = [jnp.exp(peak - top) for peak in peaks]
    denominator = fresh_scale * fresh_total + own_scale * own_total
    for scale, total in zip(scales, totals):
        denominator = denominator + scale * total
    numerator = fresh_scale * fresh_sum + own_scale * own_sum
    drain(sums_in.at[pl.ds(3, 2)], s4_recv.at[4])
    for k in range(2):
        numerator = numerator + scales[k] * sums_in[3 + k].astype(F32)
    inverse = 1.0 / denominator
    for h, lanes in enumerate(HALVES):
        cut = slice(lanes.start, lanes.start + lanes.size)
        piece = numerator[:, cut]
        drain(sums_in.at[pl.ds(5, 2), :, lanes], s4_recv.at[5 + h])
        for n in range(2):
            piece = piece + scales[2 + n] * sums_in[5 + n, :, cut].astype(F32)
        out[:, :, :, :, cut] = (piece * inverse).astype(BF16).reshape(2, 1, 2, 16, lanes.size)

    drain(outgoing.at[pl.ds(0, 7)], s1_send)
    drain(all_queries.at[pl.ds(0, 7)], q_send)
    for c in range(chunks):
        drain(gathered[c].at[pl.ds(0, 7)], s2_send.at[c])
        drain(picked[c].at[pl.ds(0, 7)], s3_send.at[c])
    drain(stats, st_send)
    drain(sums.at[pl.ds(0, 7)], s4_send)


def local(prefill_latent, stretch_page, page_table, page_list, lengths, queries, new_latent):
    vmem = pl.BlockSpec(memory_space=pltpu.VMEM)
    hbm = pl.BlockSpec(memory_space=pltpu.HBM)
    dma = pltpu.SemaphoreType.DMA
    chunks = len(CHUNKS)
    blocks = [pltpu.VMEM((8, 64, width), BF16) for _, width in CHUNKS]
    return pl.pallas_call(
        kernel,
        out_shape=(
            jax.ShapeDtypeStruct((2, 1, 2, 16, LAT), BF16),
            jax.ShapeDtypeStruct((8, 8, LATW), BF16),
        ),
        in_specs=[hbm] * 8,
        out_specs=(vmem, vmem),
        scratch_shapes=[
            pltpu.VMEM((8, 16, LATW), BF16),
            pltpu.SMEM((512,), I32),
            pltpu.VMEM((1, 512), I32),
            pltpu.VMEM((2, 512), I32),
            pltpu.SMEM((8, 64), I32),
            pltpu.SMEM((64,), I32),
            pltpu.VMEM((2, 1, 2, LATW), BF16),
            pltpu.VMEM((8, 16, 384), BF16),
            pltpu.VMEM((8, 16, 384), BF16),
            pltpu.VMEM((8, 2, 2, 16, LATW), BF16),
            pltpu.VMEM((512, 512), BF16),
            pltpu.VMEM((8, 64, LAT), BF16),
            pltpu.VMEM((8, 64, LAT), BF16),
            pltpu.VMEM((8, 8, 128), F32),
            pltpu.VMEM((8, 8, 128), F32),
            dma((8,)), dma, dma, dma((chunks,)), dma((chunks, 3)),
            dma((chunks,)), dma((chunks,)), dma, dma, dma, dma((7,)), dma,
            *blocks, *blocks, *blocks,
        ],
        compiler_params=pltpu.CompilerParams(
            collective_id=0, has_side_effects=True, vmem_limit_bytes=24 * 1024 * 1024
        ),
        name="place_and_attend",
    )(*[pltpu.with_memory_space_constraint(x, pltpu.HBM) for x in (
        prefill_latent, stretch_page, stretch_page.reshape(1, 512), page_table.T, page_list, lengths,
        queries, new_latent)]
    )


def solution(mesh):
    in_specs = (
        P("pages", None, None),
        P(),
        P(),
        P(),
        P(),
        P(None, "pages", None, "heads", None),
        P(None, "pages", None, None),
    )
    out_specs = (P(None, "pages", None, "heads", None), P("pages", "heads", None))
    return jax.shard_map(local, mesh=mesh, in_specs=in_specs, out_specs=out_specs, check_vma=False)
```

```python
import jax
import jax.numpy as jnp
from jax import lax
from jax.experimental import pallas as pl
from jax.experimental.pallas import tpu as pltpu
from jax.sharding import PartitionSpec as P

LAT = 512
LATW = 576
PAGE = 64
NY = 8
NQ = 8
NZ = 8
SHARE = 8
WIDE = 640
CHUNKS = ((512, 128), (0, 128), (128, 256), (384, 128))
SOFTMAX_SCALE = 192.0 ** (-0.5)
MASKED_SCORE = -1e30
F32 = jnp.float32
BF16 = jnp.bfloat16
I32 = jnp.int32
FIRST = 3
ORDER = (
    ("near", 0),
    ("near", 1),
    ("near", 2),
    ("far", 0),
    ("far", 1),
    ("near", 3),
    ("far", 2),
    ("pass", 0),
    ("pass", 1),
    ("far", 3),
    ("pass", 2),
    ("pass", 3),
)
HALVES = (pl.ds(0, 256), pl.ds(256, 256))
DEPTH_ORDER = (4, 3, 5, 2, 6, 1, 7)
BATCHES = ((3, 5, 4, 2), (6, 1, 7, 0))


def iota(shape, dim):
    return lax.broadcasted_iota(I32, shape, dim)


def dot(a, b):
    return jnp.dot(a, b, preferred_element_type=F32)


def dot_last(a, b):
    return lax.dot_general(a, b, (((1,), (1,)), ((), ())), preferred_element_type=F32)


def hot(mask):
    return mask.astype(F32).astype(BF16)


def kernel(
    prefill_hbm, stretch_hbm, stretch_row_hbm, table_hbm, plist_hbm, lengths_hbm, queries_hbm, fresh_hbm,
    out, cache,
    pages, stretch, stretch_row, table, plist, lengths, fresh,
    outgoing, incoming, all_queries, picks,
    sums, sums_in, stats, stats_in,
    load_sem, s1_send, s1_recv, s2_send, s2_recv,
    s3_send, s3_recv, q_send, q_recv, s4_send, s4_recv, st_send, *blocks,
):
    chunks = len(CHUNKS)
    gathered, picked, keys = blocks[:chunks], blocks[chunks : 2 * chunks], blocks[2 * chunks :]
    p = lax.axis_index("pages")
    z = lax.axis_index("heads")
    y = p // NQ
    q = lax.rem(p, NQ)
    core = lax.rem(q, 2)

    def in_row(i):
        return (y * NQ + i, z)

    def in_column(step):
        return (lax.rem(y + NY + step, NY) * NQ + q, z)

    def in_depth(i):
        return (p, i)

    loads = []
    sources = (
        (prefill_hbm.at[:, pl.ds(pl.multiple_of((z // 2) * 16, 16), 16), :], pages),
        (stretch_hbm, stretch),
        (table_hbm, table),
        (queries_hbm.at[:, 0], all_queries.at[z]),
        (stretch_row_hbm, stretch_row),
        (plist_hbm.at[pl.ds(pl.multiple_of(y * NQ, NQ), NQ), :], plist),
        (lengths_hbm, lengths),
        (fresh_hbm, fresh),
    )
    for n, (src, dst) in enumerate(sources):
        copy = pltpu.make_async_copy(src, dst, load_sem.at[n])
        copy.start()
        loads.append(copy)

    barrier = pltpu.get_barrier_semaphore()
    row_peers = [lax.rem(q + o, NQ) for o in range(1, NQ)]
    depth_peers = [lax.rem(z + o, NZ) for o in DEPTH_ORDER]
    targets = [in_row(i) for i in row_peers] + [in_column(d) for d in (1, -1, 2, -2)]
    targets += [in_depth(i) for i in depth_peers]
    for target in targets:
        pl.semaphore_signal(barrier, inc=1, device_id=target, device_id_type=pl.DeviceIdType.MESH)

    def drain(ref, sem):
        pltpu.make_async_copy(ref, ref, sem).wait()

    def remote(src, dst, send, recv, target):
        return pltpu.make_async_remote_copy(
            src_ref=src, dst_ref=dst, send_sem=send, recv_sem=recv,
            device_id=target, device_id_type=pl.DeviceIdType.MESH,
        )

    for copy in loads[0:3]:
        copy.wait()
    shift = table[0:1, 0:1]
    lane = iota((1, 128), 1)
    page_of_lane = jnp.zeros((1, 128), I32)
    for k in range(8):
        page_of_lane = jnp.where(lane // 16 == k, stretch[p * 8 + k], page_of_lane)
    residue = (page_of_lane + shift) & 7
    row = iota((128, 128), 0)
    col = iota((128, 128), 1)
    chosen = jnp.logical_and(residue == row // 16, (col & 15) == (row & 7) + 8 * lax.rem(z, 2))
    ordered = dot(hot(chosen), pages[...].reshape(128, LATW)).astype(BF16).astype(F32)
    second = (iota((128, 256), 0) & 8) == 8
    body = jnp.where(second, ordered[:, 256:512], ordered[:, 0:256]).astype(BF16)
    outgoing[:, :, 0:256] = body.reshape(8, 16, 256)
    outgoing[:, :, 256:320] = ordered[:, 512:576].astype(BF16).reshape(8, 16, 64)
    outgoing[:, :, 320:384] = jnp.zeros((8, 16, 64), BF16)

    pl.semaphore_wait(barrier, len(targets))

    for i in row_peers:
        copy = remote(outgoing.at[i], incoming.at[q], s1_send, s1_recv, in_row(i))
        copy.start()
    incoming[q] = outgoing[q]

    for copy in loads[3:]:
        copy.wait()
    for i in depth_peers:
        remote(all_queries.at[z], all_queries.at[z], q_send, q_recv, in_depth(i)).start()
    drain(incoming.at[pl.ds(0, 7)], s1_recv)
    arrived = incoming[...].astype(F32)
    whole = jnp.concatenate([arrived[:, 0:8, 0:256], arrived[:, 8:16, 0:256], arrived[:, 0:8, 256:384]], axis=2)
    whole = whole.reshape(64, WIDE).astype(BF16)
    for c, (start, width) in enumerate(CHUNKS):
        gathered[c][y] = whole[:, start : start + width]


    def along(c, kind, block, rows, step):
        view = gathered[c].at[lax.rem(block + NY, NY), pl.ds(rows[0], rows[1]), :]
        remote(view, view, s2_send.at[c], s2_recv.at[c, min(kind, 2)], in_column(step)).start()

    def start_near(c):
        along(c, 0, y, (0, 64), 2)
        along(c, 1, y, (0, 64), -2)
        along(c, 2, y, (0, 64), 1)
        along(c, 3, y, (0, 64), -1)

    def start_far(c):
        drain(gathered[c].at[0], s2_recv.at[c, 0])
        along(c, 4, y - 2, (0, 64), 1)
        along(c, 6, y - 2, (0, 32), 2)
        drain(gathered[c].at[0], s2_recv.at[c, 1])
        along(c, 5, y + 2, (0, 64), -1)
        along(c, 7, y + 2, (32, 32), -2)

    def part(ref, i, c):
        return ref[c].at[i]

    def hand(c, m, parity):
        i = lax.rem(q // 2 + m, 4) * 2 + parity
        copy = remote(
            part(picked, i, c), part(keys, q, c), s3_send.at[c], s3_recv.at[c], in_row(i)
        )
        copy.start()

    def hand_sibling(c):
        i = q + 1 - 2 * core
        copy = remote(part(picked, i, c), part(keys, q, c), s3_send.at[c], s3_recv.at[c], in_row(i))
        copy.start()

    def hand_core(c, parity):
        for m in (2, 1, 3):
            hand(c, m, parity)

    def pass_on(c):
        drain(gathered[c].at[pl.ds(0, 5)], s2_recv.at[c, 2])
        width = CHUNKS[c][1]
        have = gathered[c][...].reshape(512, width)
        picked[c][...] = dot(picks[...], have).astype(BF16).reshape(8, 64, width)
        for m in (2, 1, 3):
            hand(c, m, 0)
            hand(c, m, 1)
        hand_sibling(c)
        keys[c][q] = picked[c][q]

    start = {"near": start_near, "far": start_far, "pass": pass_on}
    for kind, c in ORDER[:FIRST]:
        start[kind](c)

    numbers = stretch_row[...]
    mine = ((numbers + shift) & 7) == q
    parts = jnp.where(iota((8, 512), 0) == 0, numbers // 8, numbers & 7)
    parts = jnp.where(mine, parts, 0).astype(F32).astype(BF16)
    same = hot(iota((512, 512), 0) // 8 == iota((512, 512), 1) // 8)
    found = dot(parts, same)
    have_key = (found[0:1, :] * 64.0 + found[1:2, :] * 8.0).astype(I32) + (iota((1, 512), 1) & 7)
    for half in range(2):
        first = jnp.zeros((256, 1), I32)
        dest = iota((256, 1), 0) // 64
        for i in range(4):
            first = jnp.where(dest == i, plist[half * 4 + i, 0], first)
        first = first + ((q - shift - first) & 7)
        inner = iota((256, 1), 0) & 63
        want = (first + 8 * (inner // 8)) * 8 + (inner & 7)
        picks[pl.ds(half * 256, 256), :] = hot(want == have_key)

    for kind, c in ORDER[FIRST:]:
        start[kind](c)

    own_queries = all_queries[z].reshape(64, LATW)
    fresh_rows = jnp.zeros((16, LATW), F32)
    fresh_index = iota((16, LATW), 0)
    for m in range(4):
        one = fresh[m // 2, 0, m % 2 : m % 2 + 1, :].astype(F32)
        fresh_rows = jnp.where(fresh_index == m, one, fresh_rows)
    fresh_rows = fresh_rows.astype(BF16)
    fresh_scores = dot_last(own_queries, fresh_rows) * SOFTMAX_SCALE
    seen = iota((64, 16), 1) <= iota((64, 16), 0) // 16
    fresh_peak = jnp.max(jnp.where(seen, fresh_scores, MASKED_SCORE), axis=1, keepdims=True)
    fresh_weight = jnp.where(seen, jnp.exp(fresh_scores - fresh_peak), 0.0)
    fresh_total = jnp.sum(fresh_weight, axis=1, keepdims=True)
    fresh_sum = dot(fresh_weight.astype(BF16), fresh_rows[:, 0:LAT])

    def joined(refs):
        order = sorted(range(chunks), key=lambda c: CHUNKS[c][0])
        return jnp.concatenate([refs[c][...].reshape(512, CHUNKS[c][1]) for c in order], axis=1)

    slot = iota((64, 512), 0) // 8
    here = jnp.logical_and(table[0:1, :] == p, table[1:2, :] == slot)
    number = jnp.where(here, iota((64, 512), 1), 0).astype(F32)
    want = jnp.sum(number, axis=1, keepdims=True).astype(I32) * 8 + (iota((64, 1), 0) & 7)
    pick = hot(want == have_key)
    cache[...] = dot(pick, joined(gathered)[:, 0:LATW]).reshape(8, 8, LATW).astype(BF16)

    begin = plist[q, 0]
    token = iota((1, 512), 1)
    position = ((token // 64 - shift - begin) & 7) + 8 * ((token & 63) // 8)
    live = position * PAGE + z * SHARE + (token & 7) < lengths[p]

    drain(all_queries.at[pl.ds(0, 7)], q_recv)
    for c in range(chunks):
        drain(keys[c].at[pl.ds(0, 7)], s3_recv.at[c])
    latents = joined(keys)
    narrow = latents[:, 0:LATW]
    values = latents[:, 0:LAT]


    def send(src, dst, sem, target):
        remote(src, dst, s4_send, s4_recv.at[sem], in_depth(target)).start()

    def send_stat(src, dst, sem, target):
        remote(stats.at[src], stats_in.at[dst], st_send, s4_recv.at[sem], in_depth(target)).start()

    def stat_rows(pairs):
        lane = iota((64, 128), 1)
        block = jnp.zeros((64, 128), F32)
        for k, (peak, total) in enumerate(pairs):
            block = jnp.where(lane == 8 * k, peak, jnp.where(lane == 8 * k + 1, total, block))
        rows = jnp.transpose(block)
        return [jnp.concatenate([rows[8 * k : 8 * k + 8]] * 2, axis=1) for k in range(len(pairs))]

    def weigh(offsets):
        asked = jnp.concatenate([all_queries[depth[o]].reshape(64, LATW) for o in offsets], axis=0)
        scores = dot_last(asked, narrow) * SOFTMAX_SCALE
        scores = jnp.where(live, scores, MASKED_SCORE)
        peak = jnp.max(scores, axis=1, keepdims=True)
        weight = jnp.where(live, jnp.exp(scores - peak), 0.0)
        total = jnp.sum(weight, axis=1, keepdims=True)
        pairs = {o: (peak[64 * k : 64 * k + 64], total[64 * k : 64 * k + 64]) for k, o in enumerate(offsets)}
        return weight.astype(BF16), pairs

    def add_up(offsets, weight, pairs):
        summed = dot(weight, values)
        return {o: (summed[64 * k : 64 * k + 64],) + pairs[o] for k, o in enumerate(offsets)}

    depth = [lax.rem(z + o, NZ) for o in range(NZ)]
    weight, pairs = weigh(BATCHES[0])
    stats[3], stats[5], stats[4] = stat_rows([pairs[o] for o in (3, 5, 4)])
    send_stat(3, 0, 0, depth[1])
    send_stat(5, 2, 0, depth[7])
    send_stat(4, 1, 0, depth[2])
    send_stat(4, 3, 0, depth[6])
    terms = add_up(BATCHES[0], weight, pairs)
    for o in (3, 5, 4):
        sums[o] = terms[o][0].astype(BF16)
    top_rows, low_rows = pl.ds(0, 32), pl.ds(32, 32)
    for h, lanes in enumerate(HALVES):
        send(sums.at[3, :, lanes], sums_in.at[0, :, lanes], 2 + h, depth[1])
        send(sums.at[5, :, lanes], sums_in.at[1, :, lanes], 2 + h, depth[7])
        send(sums.at[4, top_rows, lanes], sums_in.at[2, top_rows, lanes], 2 + h, depth[2])
        send(sums.at[4, low_rows, lanes], sums_in.at[2, low_rows, lanes], 2 + h, depth[6])
    ahead = terms[2]
    weight, pairs = weigh(BATCHES[1])
    stats[1], stats[7] = stat_rows([pairs[o] for o in (1, 7)])
    send_stat(1, 4, 1, depth[1])
    send_stat(7, 5, 1, depth[7])
    terms = add_up(BATCHES[1], weight, pairs)
    behind = terms[6]
    for o in (1, 7):
        sums[o] = terms[o][0].astype(BF16)
    send(sums.at[1], sums_in.at[3], 4, depth[1])
    send(sums.at[7], sums_in.at[4], 4, depth[7])
    own_sum, own_peak, own_total = terms[0]

    def columns(blocks):
        filled = jnp.concatenate(blocks + [jnp.zeros((128 - 8 * len(blocks), 128), F32)], axis=0)
        return jnp.transpose(filled)[0:64, :]

    def relay_scales(n, own, first_rows):
        _, own_peak, own_total = own
        inside = iota((64, 1), 0) < 32
        if not first_rows:
            inside = jnp.logical_not(inside)
        full_peak, full_total, half_peak, half_total = [spread[:, 16 * n + k : 16 * n + k + 1] for k in (0, 1, 8, 9)]
        half_peak = jnp.where(inside, half_peak, MASKED_SCORE)
        half_total = jnp.where(inside, half_total, 0.0)
        peak = jnp.maximum(jnp.maximum(own_peak, full_peak), half_peak)
        own_scale = jnp.exp(own_peak - peak)
        full_scale = jnp.exp(full_peak - peak)
        half_scale = jnp.exp(half_peak - peak)
        total = own_scale * own_total + full_scale * full_total + half_scale * half_total
        return (peak, total), (own_scale, full_scale, half_scale)

    routes = ((ahead, 0, True), (behind, 1, False))
    drain(stats_in.at[pl.ds(0, 4)], s4_recv.at[0])
    spread = columns([stats_in[k] for k in range(4)])
    merged_pairs, route_scales = zip(*[relay_scales(n, own, first_rows) for n, (own, _, first_rows) in enumerate(routes)])
    stats[2], stats[6] = stat_rows(merged_pairs)
    send_stat(2, 6, 1, depth[2])
    send_stat(6, 7, 1, depth[6])
    for h, lanes in enumerate(HALVES):
        cut = slice(lanes.start, lanes.start + lanes.size)
        drain(sums_in.at[pl.ds(0, 3), :, lanes], s4_recv.at[2 + h])
        for n, (own, full, first_rows) in enumerate(routes):
            own_scale, full_scale, half_scale = route_scales[n]
            merged = own_scale * own[0][:, cut] + full_scale * sums_in[full, :, cut].astype(F32)
            rows = slice(0, 32) if first_rows else slice(32, 64)
            extra = half_scale[rows] * sums_in[2, rows, cut].astype(F32)
            pieces = [merged[0:32], merged[32:64]]
            k = 0 if first_rows else 1
            pieces[k] = pieces[k] + extra
            o = 2 if first_rows else 6
            sums[o, :, cut] = jnp.concatenate(pieces, axis=0).astype(BF16)
            send(sums.at[o, :, lanes], sums_in.at[5 + n, :, lanes], 5 + h, depth[o])

    drain(stats_in.at[pl.ds(4, 4)], s4_recv.at[1])
    spread = columns([stats_in[k] for k in (4, 5, 6, 7)])
    peaks = [spread[:, 8 * k : 8 * k + 1] for k in range(4)]
    totals = [spread[:, 8 * k + 1 : 8 * k + 2] for k in range(4)]
    top = jnp.maximum(own_peak, fresh_peak)
    for peak in peaks:
        top = jnp.maximum(top, peak)
    fresh_scale = jnp.exp(fresh_peak - top)
    own_scale = jnp.exp(own_peak - top)
    scales = [jnp.exp(peak - top) for peak in peaks]
    denominator = fresh_scale * fresh_total + own_scale * own_total
    for scale, total in zip(scales, totals):
        denominator = denominator + scale * total
    numerator = fresh_scale * fresh_sum + own_scale * own_sum
    drain(sums_in.at[pl.ds(3, 2)], s4_recv.at[4])
    for k in range(2):
        numerator = numerator + scales[k] * sums_in[3 + k].astype(F32)
    inverse = 1.0 / denominator
    for h, lanes in enumerate(HALVES):
        cut = slice(lanes.start, lanes.start + lanes.size)
        piece = numerator[:, cut]
        drain(sums_in.at[pl.ds(5, 2), :, lanes], s4_recv.at[5 + h])
        for n in range(2):
            piece = piece + scales[2 + n] * sums_in[5 + n, :, cut].astype(F32)
        out[:, :, :, :, cut] = (piece * inverse).astype(BF16).reshape(2, 1, 2, 16, lanes.size)

    drain(outgoing.at[pl.ds(0, 7)], s1_send)
    drain(all_queries.at[pl.ds(0, 7)], q_send)
    for c in range(chunks):
        drain(gathered[c].at[pl.ds(0, 7)], s2_send.at[c])
        drain(picked[c].at[pl.ds(0, 7)], s3_send.at[c])
    drain(stats, st_send)
    drain(sums.at[pl.ds(0, 7)], s4_send)


def local(prefill_latent, stretch_page, page_table, page_list, lengths, queries, new_latent):
    vmem = pl.BlockSpec(memory_space=pltpu.VMEM)
    hbm = pl.BlockSpec(memory_space=pltpu.HBM)
    dma = pltpu.SemaphoreType.DMA
    chunks = len(CHUNKS)
    blocks = [pltpu.VMEM((8, 64, width), BF16) for _, width in CHUNKS]
    return pl.pallas_call(
        kernel,
        out_shape=(
            jax.ShapeDtypeStruct((2, 1, 2, 16, LAT), BF16),
            jax.ShapeDtypeStruct((8, 8, LATW), BF16),
        ),
        in_specs=[hbm] * 8,
        out_specs=(vmem, vmem),
        scratch_shapes=[
            pltpu.VMEM((8, 16, LATW), BF16),
            pltpu.SMEM((512,), I32),
            pltpu.VMEM((1, 512), I32),
            pltpu.VMEM((2, 512), I32),
            pltpu.SMEM((8, 64), I32),
            pltpu.SMEM((64,), I32),
            pltpu.VMEM((2, 1, 2, LATW), BF16),
            pltpu.VMEM((8, 16, 384), BF16),
            pltpu.VMEM((8, 16, 384), BF16),
            pltpu.VMEM((8, 2, 2, 16, LATW), BF16),
            pltpu.VMEM((512, 512), BF16),
            pltpu.VMEM((8, 64, LAT), BF16),
            pltpu.VMEM((8, 64, LAT), BF16),
            pltpu.VMEM((8, 8, 128), F32),
            pltpu.VMEM((8, 8, 128), F32),
            dma((8,)), dma, dma, dma((chunks,)), dma((chunks, 3)),
            dma((chunks,)), dma((chunks,)), dma, dma, dma, dma((7,)), dma,
            *blocks, *blocks, *blocks,
        ],
        compiler_params=pltpu.CompilerParams(
            collective_id=0, has_side_effects=True, vmem_limit_bytes=24 * 1024 * 1024
        ),
        name="place_and_attend",
    )(*[pltpu.with_memory_space_constraint(x, pltpu.HBM) for x in (
        prefill_latent, stretch_page, stretch_page.reshape(1, 512), page_table.T, page_list, lengths,
        queries, new_latent)]
    )


def solution(mesh):
    in_specs = (
        P("pages", None, None),
        P(),
        P(),
        P(),
        P(),
        P(None, "pages", None, "heads", None),
        P(None, "pages", None, None),
    )
    out_specs = (P(None, "pages", None, "heads", None), P("pages", "heads", None))
    return jax.shard_map(local, mesh=mesh, in_specs=in_specs, out_specs=out_specs, check_vma=False)
```

```python
import jax
import jax.numpy as jnp
from jax import lax
from jax.experimental import pallas as pl
from jax.experimental.pallas import tpu as pltpu
from jax.sharding import PartitionSpec as P

LAT = 512
LATW = 576
PAGE = 64
NY = 8
NQ = 8
NZ = 8
SHARE = 8
WIDE = 640
CHUNKS = ((512, 128), (0, 128), (128, 256), (384, 128))
SOFTMAX_SCALE = 192.0 ** (-0.5)
MASKED_SCORE = -1e30
F32 = jnp.float32
BF16 = jnp.bfloat16
I32 = jnp.int32
FIRST = 3
ORDER = (
    ("near", 0),
    ("near", 1),
    ("near", 2),
    ("far", 0),
    ("far", 1),
    ("near", 3),
    ("far", 2),
    ("pass", 0),
    ("pass", 1),
    ("far", 3),
    ("pass", 2),
    ("pass", 3),
)
HALVES = (pl.ds(0, 256), pl.ds(256, 256))
DEPTH_ORDER = (4, 3, 5, 2, 6, 1, 7)
BATCHES = ((3, 5, 4, 2), (6, 1, 7, 0))


def iota(shape, dim):
    return lax.broadcasted_iota(I32, shape, dim)


def dot(a, b):
    return jnp.dot(a, b, preferred_element_type=F32)


def dot_last(a, b):
    return lax.dot_general(a, b, (((1,), (1,)), ((), ())), preferred_element_type=F32)


def hot(mask):
    return mask.astype(F32).astype(BF16)


def kernel(
    prefill_hbm, stretch_hbm, stretch_row_hbm, table_hbm, plist_hbm, lengths_hbm, queries_hbm, fresh_hbm,
    out, cache,
    pages, stretch, stretch_row, table, plist, lengths, fresh,
    outgoing, incoming, all_queries, picks,
    sums, sums_in, stats, stats_in,
    load_sem, s1_send, s1_recv, s2_send, s2_recv,
    s3_send, s3_recv, q_send, q_recv, s4_send, s4_recv, st_send, *blocks,
):
    chunks = len(CHUNKS)
    gathered, picked, keys = blocks[:chunks], blocks[chunks : 2 * chunks], blocks[2 * chunks :]
    p = lax.axis_index("pages")
    z = lax.axis_index("heads")
    y = p // NQ
    q = lax.rem(p, NQ)
    core = lax.rem(q, 2)

    def in_row(i):
        return (y * NQ + i, z)

    def in_column(step):
        return (lax.rem(y + NY + step, NY) * NQ + q, z)

    def in_depth(i):
        return (p, i)

    loads = []
    sources = (
        (prefill_hbm.at[:, pl.ds(pl.multiple_of((z // 2) * 16, 16), 16), :], pages),
        (stretch_hbm, stretch),
        (table_hbm, table),
        (queries_hbm.at[:, 0], all_queries.at[z]),
        (stretch_row_hbm, stretch_row),
        (plist_hbm.at[pl.ds(pl.multiple_of(y * NQ, NQ), NQ), :], plist),
        (lengths_hbm, lengths),
        (fresh_hbm, fresh),
    )
    for n, (src, dst) in enumerate(sources):
        copy = pltpu.make_async_copy(src, dst, load_sem.at[n])
        copy.start()
        loads.append(copy)

    barrier = pltpu.get_barrier_semaphore()
    row_peers = [lax.rem(q + o, NQ) for o in (4, 3, 5, 2, 6, 1, 7)]
    depth_peers = [lax.rem(z + o, NZ) for o in DEPTH_ORDER]
    targets = [in_row(i) for i in row_peers] + [in_column(d) for d in (1, -1, 2, -2)]
    targets += [in_depth(i) for i in depth_peers]
    for target in targets:
        pl.semaphore_signal(barrier, inc=1, device_id=target, device_id_type=pl.DeviceIdType.MESH)

    def drain(ref, sem):
        pltpu.make_async_copy(ref, ref, sem).wait()

    def remote(src, dst, send, recv, target):
        return pltpu.make_async_remote_copy(
            src_ref=src, dst_ref=dst, send_sem=send, recv_sem=recv,
            device_id=target, device_id_type=pl.DeviceIdType.MESH,
        )

    for copy in loads[0:3]:
        copy.wait()
    shift = table[0:1, 0:1]
    lane = iota((1, 128), 1)
    page_of_lane = jnp.zeros((1, 128), I32)
    for k in range(8):
        page_of_lane = jnp.where(lane // 16 == k, stretch[p * 8 + k], page_of_lane)
    residue = (page_of_lane + shift) & 7
    row = iota((128, 128), 0)
    col = iota((128, 128), 1)
    chosen = jnp.logical_and(residue == row // 16, (col & 15) == (row & 7) + 8 * lax.rem(z, 2))
    ordered = dot(hot(chosen), pages[...].reshape(128, LATW)).astype(BF16).astype(F32)
    second = (iota((128, 256), 0) & 8) == 8
    body = jnp.where(second, ordered[:, 256:512], ordered[:, 0:256]).astype(BF16)
    outgoing[:, :, 0:256] = body.reshape(8, 16, 256)
    outgoing[:, :, 256:320] = ordered[:, 512:576].astype(BF16).reshape(8, 16, 64)
    outgoing[:, :, 320:384] = jnp.zeros((8, 16, 64), BF16)

    pl.semaphore_wait(barrier, len(targets))

    for i in row_peers:
        copy = remote(outgoing.at[i], incoming.at[q], s1_send, s1_recv, in_row(i))
        copy.start()
    incoming[q] = outgoing[q]

    for copy in loads[3:]:
        copy.wait()
    for i in depth_peers:
        remote(all_queries.at[z], all_queries.at[z], q_send, q_recv, in_depth(i)).start()
    drain(incoming.at[pl.ds(0, 7)], s1_recv)
    arrived = incoming[...].astype(F32)
    whole = jnp.concatenate([arrived[:, 0:8, 0:256], arrived[:, 8:16, 0:256], arrived[:, 0:8, 256:384]], axis=2)
    whole = whole.reshape(64, WIDE).astype(BF16)
    for c, (start, width) in enumerate(CHUNKS):
        gathered[c][y] = whole[:, start : start + width]


    def along(c, kind, block, rows, step):
        view = gathered[c].at[lax.rem(block + NY, NY), pl.ds(rows[0], rows[1]), :]
        remote(view, view, s2_send.at[c], s2_recv.at[c, min(kind, 2)], in_column(step)).start()

    def start_near(c):
        along(c, 0, y, (0, 64), 2)
        along(c, 1, y, (0, 64), -2)
        along(c, 2, y, (0, 64), 1)
        along(c, 3, y, (0, 64), -1)

    def start_far(c):
        drain(gathered[c].at[0], s2_recv.at[c, 0])
        along(c, 4, y - 2, (0, 64), 1)
        along(c, 6, y - 2, (0, 32), 2)
        drain(gathered[c].at[0], s2_recv.at[c, 1])
        along(c, 5, y + 2, (0, 64), -1)
        along(c, 7, y + 2, (32, 32), -2)

    def part(ref, i, c):
        return ref[c].at[i]

    def hand(c, m, parity):
        i = lax.rem(q // 2 + m, 4) * 2 + parity
        copy = remote(
            part(picked, i, c), part(keys, q, c), s3_send.at[c], s3_recv.at[c], in_row(i)
        )
        copy.start()

    def hand_sibling(c):
        i = q + 1 - 2 * core
        copy = remote(part(picked, i, c), part(keys, q, c), s3_send.at[c], s3_recv.at[c], in_row(i))
        copy.start()

    def hand_core(c, parity):
        for m in (2, 1, 3):
            hand(c, m, parity)

    def pass_on(c):
        drain(gathered[c].at[pl.ds(0, 5)], s2_recv.at[c, 2])
        width = CHUNKS[c][1]
        have = gathered[c][...].reshape(512, width)
        picked[c][...] = dot(picks[...], have).astype(BF16).reshape(8, 64, width)
        for m in (2, 1, 3):
            hand(c, m, 0)
            hand(c, m, 1)
        hand_sibling(c)
        keys[c][q] = picked[c][q]

    start = {"near": start_near, "far": start_far, "pass": pass_on}
    for kind, c in ORDER[:FIRST]:
        start[kind](c)

    numbers = stretch_row[...]
    mine = ((numbers + shift) & 7) == q
    parts = jnp.where(iota((8, 512), 0) == 0, numbers // 8, numbers & 7)
    parts = jnp.where(mine, parts, 0).astype(F32).astype(BF16)
    same = hot(iota((512, 512), 0) // 8 == iota((512, 512), 1) // 8)
    found = dot(parts, same)
    have_key = (found[0:1, :] * 64.0 + found[1:2, :] * 8.0).astype(I32) + (iota((1, 512), 1) & 7)
    for half in range(2):
        first = jnp.zeros((256, 1), I32)
        dest = iota((256, 1), 0) // 64
        for i in range(4):
            first = jnp.where(dest == i, plist[half * 4 + i, 0], first)
        first = first + ((q - shift - first) & 7)
        inner = iota((256, 1), 0) & 63
        want = (first + 8 * (inner // 8)) * 8 + (inner & 7)
        picks[pl.ds(half * 256, 256), :] = hot(want == have_key)

    for kind, c in ORDER[FIRST:]:
        start[kind](c)

    own_queries = all_queries[z].reshape(64, LATW)
    fresh_rows = jnp.zeros((16, LATW), F32)
    fresh_index = iota((16, LATW), 0)
    for m in range(4):
        one = fresh[m // 2, 0, m % 2 : m % 2 + 1, :].astype(F32)
        fresh_rows = jnp.where(fresh_index == m, one, fresh_rows)
    fresh_rows = fresh_rows.astype(BF16)
    fresh_scores = dot_last(own_queries, fresh_rows) * SOFTMAX_SCALE
    seen = iota((64, 16), 1) <= iota((64, 16), 0) // 16
    fresh_peak = jnp.max(jnp.where(seen, fresh_scores, MASKED_SCORE), axis=1, keepdims=True)
    fresh_weight = jnp.where(seen, jnp.exp(fresh_scores - fresh_peak), 0.0)
    fresh_total = jnp.sum(fresh_weight, axis=1, keepdims=True)
    fresh_sum = dot(fresh_weight.astype(BF16), fresh_rows[:, 0:LAT])

    def joined(refs):
        order = sorted(range(chunks), key=lambda c: CHUNKS[c][0])
        return jnp.concatenate([refs[c][...].reshape(512, CHUNKS[c][1]) for c in order], axis=1)

    slot = iota((64, 512), 0) // 8
    here = jnp.logical_and(table[0:1, :] == p, table[1:2, :] == slot)
    number = jnp.where(here, iota((64, 512), 1), 0).astype(F32)
    want = jnp.sum(number, axis=1, keepdims=True).astype(I32) * 8 + (iota((64, 1), 0) & 7)
    pick = hot(want == have_key)
    cache[...] = dot(pick, joined(gathered)[:, 0:LATW]).reshape(8, 8, LATW).astype(BF16)

    begin = plist[q, 0]
    token = iota((1, 512), 1)
    position = ((token // 64 - shift - begin) & 7) + 8 * ((token & 63) // 8)
    live = position * PAGE + z * SHARE + (token & 7) < lengths[p]

    drain(all_queries.at[pl.ds(0, 7)], q_recv)
    for c in range(chunks):
        drain(keys[c].at[pl.ds(0, 7)], s3_recv.at[c])
    latents = joined(keys)
    narrow = latents[:, 0:LATW]
    values = latents[:, 0:LAT]


    def send(src, dst, sem, target):
        remote(src, dst, s4_send, s4_recv.at[sem], in_depth(target)).start()

    def send_stat(src, dst, sem, target):
        remote(stats.at[src], stats_in.at[dst], st_send, s4_recv.at[sem], in_depth(target)).start()

    def stat_rows(pairs):
        lane = iota((64, 128), 1)
        block = jnp.zeros((64, 128), F32)
        for k, (peak, total) in enumerate(pairs):
            block = jnp.where(lane == 8 * k, peak, jnp.where(lane == 8 * k + 1, total, block))
        rows = jnp.transpose(block)
        return [jnp.concatenate([rows[8 * k : 8 * k + 8]] * 2, axis=1) for k in range(len(pairs))]

    def weigh(offsets):
        asked = jnp.concatenate([all_queries[depth[o]].reshape(64, LATW) for o in offsets], axis=0)
        scores = dot_last(asked, narrow) * SOFTMAX_SCALE
        scores = jnp.where(live, scores, MASKED_SCORE)
        peak = jnp.max(scores, axis=1, keepdims=True)
        weight = jnp.where(live, jnp.exp(scores - peak), 0.0)
        total = jnp.sum(weight, axis=1, keepdims=True)
        pairs = {o: (peak[64 * k : 64 * k + 64], total[64 * k : 64 * k + 64]) for k, o in enumerate(offsets)}
        return weight.astype(BF16), pairs

    def add_up(offsets, weight, pairs):
        summed = dot(weight, values)
        return {o: (summed[64 * k : 64 * k + 64],) + pairs[o] for k, o in enumerate(offsets)}

    depth = [lax.rem(z + o, NZ) for o in range(NZ)]
    weight, pairs = weigh(BATCHES[0])
    stats[3], stats[5], stats[4] = stat_rows([pairs[o] for o in (3, 5, 4)])
    send_stat(3, 0, 0, depth[1])
    send_stat(5, 2, 0, depth[7])
    send_stat(4, 1, 0, depth[2])
    send_stat(4, 3, 0, depth[6])
    terms = add_up(BATCHES[0], weight, pairs)
    for o in (3, 5, 4):
        sums[o] = terms[o][0].astype(BF16)
    top_rows, low_rows = pl.ds(0, 32), pl.ds(32, 32)
    for h, lanes in enumerate(HALVES):
        send(sums.at[3, :, lanes], sums_in.at[0, :, lanes], 2 + h, depth[1])
        send(sums.at[5, :, lanes], sums_in.at[1, :, lanes], 2 + h, depth[7])
        send(sums.at[4, top_rows, lanes], sums_in.at[2, top_rows, lanes], 2 + h, depth[2])
        send(sums.at[4, low_rows, lanes], sums_in.at[2, low_rows, lanes], 2 + h, depth[6])
    ahead = terms[2]
    weight, pairs = weigh(BATCHES[1])
    stats[1], stats[7] = stat_rows([pairs[o] for o in (1, 7)])
    send_stat(1, 4, 1, depth[1])
    send_stat(7, 5, 1, depth[7])
    terms = add_up(BATCHES[1], weight, pairs)
    behind = terms[6]
    for o in (1, 7):
        sums[o] = terms[o][0].astype(BF16)
    send(sums.at[1], sums_in.at[3], 4, depth[1])
    send(sums.at[7], sums_in.at[4], 4, depth[7])
    own_sum, own_peak, own_total = terms[0]

    def columns(blocks):
        filled = jnp.concatenate(blocks + [jnp.zeros((128 - 8 * len(blocks), 128), F32)], axis=0)
        return jnp.transpose(filled)[0:64, :]

    def relay_scales(n, own, first_rows):
        _, own_peak, own_total = own
        inside = iota((64, 1), 0) < 32
        if not first_rows:
            inside = jnp.logical_not(inside)
        full_peak, full_total, half_peak, half_total = [spread[:, 16 * n + k : 16 * n + k + 1] for k in (0, 1, 8, 9)]
        half_peak = jnp.where(inside, half_peak, MASKED_SCORE)
        half_total = jnp.where(inside, half_total, 0.0)
        peak = jnp.maximum(jnp.maximum(own_peak, full_peak), half_peak)
        own_scale = jnp.exp(own_peak - peak)
        full_scale = jnp.exp(full_peak - peak)
        half_scale = jnp.exp(half_peak - peak)
        total = own_scale * own_total + full_scale * full_total + half_scale * half_total
        return (peak, total), (own_scale, full_scale, half_scale)

    routes = ((ahead, 0, True), (behind, 1, False))
    drain(stats_in.at[pl.ds(0, 4)], s4_recv.at[0])
    spread = columns([stats_in[k] for k in range(4)])
    merged_pairs, route_scales = zip(*[relay_scales(n, own, first_rows) for n, (own, _, first_rows) in enumerate(routes)])
    stats[2], stats[6] = stat_rows(merged_pairs)
    send_stat(2, 6, 1, depth[2])
    send_stat(6, 7, 1, depth[6])
    for h, lanes in enumerate(HALVES):
        cut = slice(lanes.start, lanes.start + lanes.size)
        drain(sums_in.at[pl.ds(0, 3), :, lanes], s4_recv.at[2 + h])
        for n, (own, full, first_rows) in enumerate(routes):
            own_scale, full_scale, half_scale = route_scales[n]
            merged = own_scale * own[0][:, cut] + full_scale * sums_in[full, :, cut].astype(F32)
            rows = slice(0, 32) if first_rows else slice(32, 64)
            extra = half_scale[rows] * sums_in[2, rows, cut].astype(F32)
            pieces = [merged[0:32], merged[32:64]]
            k = 0 if first_rows else 1
            pieces[k] = pieces[k] + extra
            o = 2 if first_rows else 6
            sums[o, :, cut] = jnp.concatenate(pieces, axis=0).astype(BF16)
            send(sums.at[o, :, lanes], sums_in.at[5 + n, :, lanes], 5 + h, depth[o])

    drain(stats_in.at[pl.ds(4, 4)], s4_recv.at[1])
    spread = columns([stats_in[k] for k in (4, 5, 6, 7)])
    peaks = [spread[:, 8 * k : 8 * k + 1] for k in range(4)]
    totals = [spread[:, 8 * k + 1 : 8 * k + 2] for k in range(4)]
    top = jnp.maximum(own_peak, fresh_peak)
    for peak in peaks:
        top = jnp.maximum(top, peak)
    fresh_scale = jnp.exp(fresh_peak - top)
    own_scale = jnp.exp(own_peak - top)
    scales = [jnp.exp(peak - top) for peak in peaks]
    denominator = fresh_scale * fresh_total + own_scale * own_total
    for scale, total in zip(scales, totals):
        denominator = denominator + scale * total
    numerator = fresh_scale * fresh_sum + own_scale * own_sum
    drain(sums_in.at[pl.ds(3, 2)], s4_recv.at[4])
    for k in range(2):
        numerator = numerator + scales[k] * sums_in[3 + k].astype(F32)
    inverse = 1.0 / denominator
    for h, lanes in enumerate(HALVES):
        cut = slice(lanes.start, lanes.start + lanes.size)
        piece = numerator[:, cut]
        drain(sums_in.at[pl.ds(5, 2), :, lanes], s4_recv.at[5 + h])
        for n in range(2):
            piece = piece + scales[2 + n] * sums_in[5 + n, :, cut].astype(F32)
        out[:, :, :, :, cut] = (piece * inverse).astype(BF16).reshape(2, 1, 2, 16, lanes.size)

    drain(outgoing.at[pl.ds(0, 7)], s1_send)
    drain(all_queries.at[pl.ds(0, 7)], q_send)
    for c in range(chunks):
        drain(gathered[c].at[pl.ds(0, 7)], s2_send.at[c])
        drain(picked[c].at[pl.ds(0, 7)], s3_send.at[c])
    drain(stats, st_send)
    drain(sums.at[pl.ds(0, 7)], s4_send)


def local(prefill_latent, stretch_page, page_table, page_list, lengths, queries, new_latent):
    vmem = pl.BlockSpec(memory_space=pltpu.VMEM)
    hbm = pl.BlockSpec(memory_space=pltpu.HBM)
    dma = pltpu.SemaphoreType.DMA
    chunks = len(CHUNKS)
    blocks = [pltpu.VMEM((8, 64, width), BF16) for _, width in CHUNKS]
    return pl.pallas_call(
        kernel,
        out_shape=(
            jax.ShapeDtypeStruct((2, 1, 2, 16, LAT), BF16),
            jax.ShapeDtypeStruct((8, 8, LATW), BF16),
        ),
        in_specs=[hbm] * 8,
        out_specs=(vmem, vmem),
        scratch_shapes=[
            pltpu.VMEM((8, 16, LATW), BF16),
            pltpu.SMEM((512,), I32),
            pltpu.VMEM((1, 512), I32),
            pltpu.VMEM((2, 512), I32),
            pltpu.SMEM((8, 64), I32),
            pltpu.SMEM((64,), I32),
            pltpu.VMEM((2, 1, 2, LATW), BF16),
            pltpu.VMEM((8, 16, 384), BF16),
            pltpu.VMEM((8, 16, 384), BF16),
            pltpu.VMEM((8, 2, 2, 16, LATW), BF16),
            pltpu.VMEM((512, 512), BF16),
            pltpu.VMEM((8, 64, LAT), BF16),
            pltpu.VMEM((8, 64, LAT), BF16),
            pltpu.VMEM((8, 8, 128), F32),
            pltpu.VMEM((8, 8, 128), F32),
            dma((8,)), dma, dma, dma((chunks,)), dma((chunks, 3)),
            dma((chunks,)), dma((chunks,)), dma, dma, dma, dma((7,)), dma,
            *blocks, *blocks, *blocks,
        ],
        compiler_params=pltpu.CompilerParams(
            collective_id=0, has_side_effects=True, vmem_limit_bytes=24 * 1024 * 1024
        ),
        name="place_and_attend",
    )(*[pltpu.with_memory_space_constraint(x, pltpu.HBM) for x in (
        prefill_latent, stretch_page, stretch_page.reshape(1, 512), page_table.T, page_list, lengths,
        queries, new_latent)]
    )


def solution(mesh):
    in_specs = (
        P("pages", None, None),
        P(),
        P(),
        P(),
        P(),
        P(None, "pages", None, "heads", None),
        P(None, "pages", None, None),
    )
    out_specs = (P(None, "pages", None, "heads", None), P("pages", "heads", None))
    return jax.shard_map(local, mesh=mesh, in_specs=in_specs, out_specs=out_specs, check_vma=False)
```

```python
import jax
import jax.numpy as jnp
from jax import lax
from jax.experimental import pallas as pl
from jax.experimental.pallas import tpu as pltpu
from jax.sharding import PartitionSpec as P

LAT = 512
LATW = 576
PAGE = 64
NY = 8
NQ = 8
NZ = 8
SHARE = 8
WIDE = 640
CHUNKS = ((512, 128), (0, 128), (128, 256), (384, 128))
SOFTMAX_SCALE = 192.0 ** (-0.5)
MASKED_SCORE = -1e30
F32 = jnp.float32
BF16 = jnp.bfloat16
I32 = jnp.int32
FIRST = 3
ORDER = (
    ("near", 0),
    ("near", 1),
    ("near", 2),
    ("far", 0),
    ("far", 1),
    ("near", 3),
    ("far", 2),
    ("pass", 0),
    ("pass", 1),
    ("far", 3),
    ("pass", 2),
    ("pass", 3),
)
HALVES = (pl.ds(0, 256), pl.ds(256, 256))
DEPTH_ORDER = (4, 3, 5, 2, 6, 1, 7)
BATCHES = ((3, 5, 4, 2), (6, 1, 7, 0))


def iota(shape, dim):
    return lax.broadcasted_iota(I32, shape, dim)


def dot(a, b):
    return jnp.dot(a, b, preferred_element_type=F32)


def dot_last(a, b):
    return lax.dot_general(a, b, (((1,), (1,)), ((), ())), preferred_element_type=F32)


def hot(mask):
    return mask.astype(F32).astype(BF16)


def kernel(
    prefill_hbm, stretch_hbm, stretch_row_hbm, table_hbm, plist_hbm, lengths_hbm, queries_hbm, fresh_hbm,
    out, cache,
    pages, stretch, stretch_row, table, plist, lengths, fresh,
    outgoing, incoming, all_queries, picks,
    sums, sums_in, stats, stats_in,
    load_sem, s1_send, s1_recv, s2_send, s2_recv,
    s3_send, s3_recv, q_send, q_recv, s4_send, s4_recv, st_send, *blocks,
):
    chunks = len(CHUNKS)
    gathered, picked, keys = blocks[:chunks], blocks[chunks : 2 * chunks], blocks[2 * chunks :]
    p = lax.axis_index("pages")
    z = lax.axis_index("heads")
    y = p // NQ
    q = lax.rem(p, NQ)
    core = lax.rem(q, 2)

    def in_row(i):
        return (y * NQ + i, z)

    def in_column(step):
        return (lax.rem(y + NY + step, NY) * NQ + q, z)

    def in_depth(i):
        return (p, i)

    loads = []
    sources = (
        (prefill_hbm.at[:, pl.ds(pl.multiple_of((z // 2) * 16, 16), 16), :], pages),
        (stretch_hbm, stretch),
        (table_hbm, table),
        (queries_hbm.at[:, 0], all_queries.at[z]),
        (stretch_row_hbm, stretch_row),
        (plist_hbm.at[pl.ds(pl.multiple_of(y * NQ, NQ), NQ), :], plist),
        (lengths_hbm, lengths),
        (fresh_hbm, fresh),
    )
    for n, (src, dst) in enumerate(sources):
        copy = pltpu.make_async_copy(src, dst, load_sem.at[n])
        copy.start()
        loads.append(copy)

    barrier = pltpu.get_barrier_semaphore()
    row_peers = [lax.rem(q + o, NQ) for o in (4, 3, 5, 2, 6, 1, 7)]
    depth_peers = [lax.rem(z + o, NZ) for o in DEPTH_ORDER]
    targets = [in_row(i) for i in row_peers] + [in_column(d) for d in (1, -1, 2, -2)]
    targets += [in_depth(i) for i in depth_peers]
    for target in targets:
        pl.semaphore_signal(barrier, inc=1, device_id=target, device_id_type=pl.DeviceIdType.MESH)

    def drain(ref, sem):
        pltpu.make_async_copy(ref, ref, sem).wait()

    def remote(src, dst, send, recv, target):
        return pltpu.make_async_remote_copy(
            src_ref=src, dst_ref=dst, send_sem=send, recv_sem=recv,
            device_id=target, device_id_type=pl.DeviceIdType.MESH,
        )

    for copy in loads[0:3]:
        copy.wait()
    shift = table[0:1, 0:1]
    lane = iota((1, 128), 1)
    page_of_lane = jnp.zeros((1, 128), I32)
    for k in range(8):
        page_of_lane = jnp.where(lane // 16 == k, stretch[p * 8 + k], page_of_lane)
    residue = (page_of_lane + shift) & 7
    row = iota((128, 128), 0)
    col = iota((128, 128), 1)
    chosen = jnp.logical_and(residue == row // 16, (col & 15) == (row & 7) + 8 * lax.rem(z, 2))
    ordered = dot(hot(chosen), pages[...].reshape(128, LATW)).astype(BF16).astype(F32)
    second = (iota((128, 256), 0) & 8) == 8
    body = jnp.where(second, ordered[:, 256:512], ordered[:, 0:256]).astype(BF16)
    outgoing[:, :, 0:256] = body.reshape(8, 16, 256)
    outgoing[:, :, 256:320] = ordered[:, 512:576].astype(BF16).reshape(8, 16, 64)
    outgoing[:, :, 320:384] = jnp.zeros((8, 16, 64), BF16)

    pl.semaphore_wait(barrier, len(targets))

    for i in row_peers:
        copy = remote(outgoing.at[i], incoming.at[q], s1_send, s1_recv, in_row(i))
        copy.start()
    incoming[q] = outgoing[q]

    for copy in loads[3:]:
        copy.wait()
    drain(incoming.at[pl.ds(0, 7)], s1_recv)
    arrived = incoming[...].astype(F32)
    whole = jnp.concatenate([arrived[:, 0:8, 0:256], arrived[:, 8:16, 0:256], arrived[:, 0:8, 256:384]], axis=2)
    whole = whole.reshape(64, WIDE).astype(BF16)
    for c, (start, width) in enumerate(CHUNKS):
        gathered[c][y] = whole[:, start : start + width]


    def along(c, kind, block, rows, step):
        view = gathered[c].at[lax.rem(block + NY, NY), pl.ds(rows[0], rows[1]), :]
        remote(view, view, s2_send.at[c], s2_recv.at[c, min(kind, 2)], in_column(step)).start()

    def start_near(c):
        along(c, 0, y, (0, 64), 2)
        along(c, 1, y, (0, 64), -2)
        along(c, 2, y, (0, 64), 1)
        along(c, 3, y, (0, 64), -1)

    def start_far(c):
        drain(gathered[c].at[0], s2_recv.at[c, 0])
        along(c, 6, y - 2, (0, 32), 2)
        along(c, 4, y - 2, (0, 64), 1)
        drain(gathered[c].at[0], s2_recv.at[c, 1])
        along(c, 7, y + 2, (32, 32), -2)
        along(c, 5, y + 2, (0, 64), -1)

    def part(ref, i, c):
        return ref[c].at[i]

    def hand(c, m, parity):
        i = lax.rem(q // 2 + m, 4) * 2 + parity
        copy = remote(
            part(picked, i, c), part(keys, q, c), s3_send.at[c], s3_recv.at[c], in_row(i)
        )
        copy.start()

    def hand_sibling(c):
        i = q + 1 - 2 * core
        copy = remote(part(picked, i, c), part(keys, q, c), s3_send.at[c], s3_recv.at[c], in_row(i))
        copy.start()

    def hand_core(c, parity):
        for m in (2, 1, 3):
            hand(c, m, parity)

    def pass_on(c):
        drain(gathered[c].at[pl.ds(0, 5)], s2_recv.at[c, 2])
        width = CHUNKS[c][1]
        have = gathered[c][...].reshape(512, width)
        picked[c][...] = dot(picks[...], have).astype(BF16).reshape(8, 64, width)
        for m in (2, 1, 3):
            hand(c, m, 0)
            hand(c, m, 1)
        hand_sibling(c)
        keys[c][q] = picked[c][q]

    start = {"near": start_near, "far": start_far, "pass": pass_on}
    for kind, c in ORDER[:FIRST]:
        start[kind](c)

    numbers = stretch_row[...]
    mine = ((numbers + shift) & 7) == q
    parts = jnp.where(iota((8, 512), 0) == 0, numbers // 8, numbers & 7)
    parts = jnp.where(mine, parts, 0).astype(F32).astype(BF16)
    same = hot(iota((512, 512), 0) // 8 == iota((512, 512), 1) // 8)
    found = dot(parts, same)
    have_key = (found[0:1, :] * 64.0 + found[1:2, :] * 8.0).astype(I32) + (iota((1, 512), 1) & 7)
    for half in range(2):
        first = jnp.zeros((256, 1), I32)
        dest = iota((256, 1), 0) // 64
        for i in range(4):
            first = jnp.where(dest == i, plist[half * 4 + i, 0], first)
        first = first + ((q - shift - first) & 7)
        inner = iota((256, 1), 0) & 63
        want = (first + 8 * (inner // 8)) * 8 + (inner & 7)
        picks[pl.ds(half * 256, 256), :] = hot(want == have_key)

    for i in depth_peers:
        remote(all_queries.at[z], all_queries.at[z], q_send, q_recv, in_depth(i)).start()
    for kind, c in ORDER[FIRST:]:
        start[kind](c)

    own_queries = all_queries[z].reshape(64, LATW)
    fresh_rows = jnp.zeros((16, LATW), F32)
    fresh_index = iota((16, LATW), 0)
    for m in range(4):
        one = fresh[m // 2, 0, m % 2 : m % 2 + 1, :].astype(F32)
        fresh_rows = jnp.where(fresh_index == m, one, fresh_rows)
    fresh_rows = fresh_rows.astype(BF16)
    fresh_scores = dot_last(own_queries, fresh_rows) * SOFTMAX_SCALE
    seen = iota((64, 16), 1) <= iota((64, 16), 0) // 16
    fresh_peak = jnp.max(jnp.where(seen, fresh_scores, MASKED_SCORE), axis=1, keepdims=True)
    fresh_weight = jnp.where(seen, jnp.exp(fresh_scores - fresh_peak), 0.0)
    fresh_total = jnp.sum(fresh_weight, axis=1, keepdims=True)
    fresh_sum = dot(fresh_weight.astype(BF16), fresh_rows[:, 0:LAT])

    def joined(refs):
        order = sorted(range(chunks), key=lambda c: CHUNKS[c][0])
        return jnp.concatenate([refs[c][...].reshape(512, CHUNKS[c][1]) for c in order], axis=1)

    slot = iota((64, 512), 0) // 8
    here = jnp.logical_and(table[0:1, :] == p, table[1:2, :] == slot)
    number = jnp.where(here, iota((64, 512), 1), 0).astype(F32)
    want = jnp.sum(number, axis=1, keepdims=True).astype(I32) * 8 + (iota((64, 1), 0) & 7)
    pick = hot(want == have_key)
    cache[...] = dot(pick, joined(gathered)[:, 0:LATW]).reshape(8, 8, LATW).astype(BF16)

    begin = plist[q, 0]
    token = iota((1, 512), 1)
    position = ((token // 64 - shift - begin) & 7) + 8 * ((token & 63) // 8)
    live = position * PAGE + z * SHARE + (token & 7) < lengths[p]

    drain(all_queries.at[pl.ds(0, 7)], q_recv)
    for c in range(chunks):
        drain(keys[c].at[pl.ds(0, 7)], s3_recv.at[c])
    latents = joined(keys)
    narrow = latents[:, 0:LATW]
    values = latents[:, 0:LAT]


    def send(src, dst, sem, target):
        remote(src, dst, s4_send, s4_recv.at[sem], in_depth(target)).start()

    def send_stat(src, dst, sem, target):
        remote(stats.at[src], stats_in.at[dst], st_send, s4_recv.at[sem], in_depth(target)).start()

    def stat_rows(pairs):
        lane = iota((64, 128), 1)
        block = jnp.zeros((64, 128), F32)
        for k, (peak, total) in enumerate(pairs):
            block = jnp.where(lane == 8 * k, peak, jnp.where(lane == 8 * k + 1, total, block))
        rows = jnp.transpose(block)
        return [jnp.concatenate([rows[8 * k : 8 * k + 8]] * 2, axis=1) for k in range(len(pairs))]

    def weigh(offsets):
        asked = jnp.concatenate([all_queries[depth[o]].reshape(64, LATW) for o in offsets], axis=0)
        scores = dot_last(asked, narrow) * SOFTMAX_SCALE
        scores = jnp.where(live, scores, MASKED_SCORE)
        peak = jnp.max(scores, axis=1, keepdims=True)
        weight = jnp.where(live, jnp.exp(scores - peak), 0.0)
        total = jnp.sum(weight, axis=1, keepdims=True)
        pairs = {o: (peak[64 * k : 64 * k + 64], total[64 * k : 64 * k + 64]) for k, o in enumerate(offsets)}
        return weight.astype(BF16), pairs

    def add_up(offsets, weight, pairs):
        summed = dot(weight, values)
        return {o: (summed[64 * k : 64 * k + 64],) + pairs[o] for k, o in enumerate(offsets)}

    depth = [lax.rem(z + o, NZ) for o in range(NZ)]
    weight, pairs = weigh(BATCHES[0])
    stats[3], stats[5], stats[4] = stat_rows([pairs[o] for o in (3, 5, 4)])
    send_stat(3, 0, 0, depth[1])
    send_stat(5, 2, 0, depth[7])
    send_stat(4, 1, 0, depth[2])
    send_stat(4, 3, 0, depth[6])
    terms = add_up(BATCHES[0], weight, pairs)
    for o in (3, 5, 4):
        sums[o] = terms[o][0].astype(BF16)
    top_rows, low_rows = pl.ds(0, 32), pl.ds(32, 32)
    for h, lanes in enumerate(HALVES):
        send(sums.at[3, :, lanes], sums_in.at[0, :, lanes], 2 + h, depth[1])
        send(sums.at[5, :, lanes], sums_in.at[1, :, lanes], 2 + h, depth[7])
        send(sums.at[4, top_rows, lanes], sums_in.at[2, top_rows, lanes], 2 + h, depth[2])
        send(sums.at[4, low_rows, lanes], sums_in.at[2, low_rows, lanes], 2 + h, depth[6])
    ahead = terms[2]
    weight, pairs = weigh(BATCHES[1])
    stats[1], stats[7] = stat_rows([pairs[o] for o in (1, 7)])
    send_stat(1, 4, 1, depth[1])
    send_stat(7, 5, 1, depth[7])
    terms = add_up(BATCHES[1], weight, pairs)
    behind = terms[6]
    for o in (1, 7):
        sums[o] = terms[o][0].astype(BF16)
    send(sums.at[1], sums_in.at[3], 4, depth[1])
    send(sums.at[7], sums_in.at[4], 4, depth[7])
    own_sum, own_peak, own_total = terms[0]

    def columns(blocks):
        filled = jnp.concatenate(blocks + [jnp.zeros((128 - 8 * len(blocks), 128), F32)], axis=0)
        return jnp.transpose(filled)[0:64, :]

    def relay_scales(n, own, first_rows):
        _, own_peak, own_total = own
        inside = iota((64, 1), 0) < 32
        if not first_rows:
            inside = jnp.logical_not(inside)
        full_peak, full_total, half_peak, half_total = [spread[:, 16 * n + k : 16 * n + k + 1] for k in (0, 1, 8, 9)]
        half_peak = jnp.where(inside, half_peak, MASKED_SCORE)
        half_total = jnp.where(inside, half_total, 0.0)
        peak = jnp.maximum(jnp.maximum(own_peak, full_peak), half_peak)
        own_scale = jnp.exp(own_peak - peak)
        full_scale = jnp.exp(full_peak - peak)
        half_scale = jnp.exp(half_peak - peak)
        total = own_scale * own_total + full_scale * full_total + half_scale * half_total
        return (peak, total), (own_scale, full_scale, half_scale)

    routes = ((ahead, 0, True), (behind, 1, False))
    drain(stats_in.at[pl.ds(0, 4)], s4_recv.at[0])
    spread = columns([stats_in[k] for k in range(4)])
    merged_pairs, route_scales = zip(*[relay_scales(n, own, first_rows) for n, (own, _, first_rows) in enumerate(routes)])
    stats[2], stats[6] = stat_rows(merged_pairs)
    send_stat(2, 6, 1, depth[2])
    send_stat(6, 7, 1, depth[6])
    for h, lanes in enumerate(HALVES):
        cut = slice(lanes.start, lanes.start + lanes.size)
        drain(sums_in.at[pl.ds(0, 3), :, lanes], s4_recv.at[2 + h])
        for n, (own, full, first_rows) in enumerate(routes):
            own_scale, full_scale, half_scale = route_scales[n]
            merged = own_scale * own[0][:, cut] + full_scale * sums_in[full, :, cut].astype(F32)
            rows = slice(0, 32) if first_rows else slice(32, 64)
            extra = half_scale[rows] * sums_in[2, rows, cut].astype(F32)
            pieces = [merged[0:32], merged[32:64]]
            k = 0 if first_rows else 1
            pieces[k] = pieces[k] + extra
            o = 2 if first_rows else 6
            sums[o, :, cut] = jnp.concatenate(pieces, axis=0).astype(BF16)
            send(sums.at[o, :, lanes], sums_in.at[5 + n, :, lanes], 5 + h, depth[o])

    drain(stats_in.at[pl.ds(4, 4)], s4_recv.at[1])
    spread = columns([stats_in[k] for k in (4, 5, 6, 7)])
    peaks = [spread[:, 8 * k : 8 * k + 1] for k in range(4)]
    totals = [spread[:, 8 * k + 1 : 8 * k + 2] for k in range(4)]
    top = jnp.maximum(own_peak, fresh_peak)
    for peak in peaks:
        top = jnp.maximum(top, peak)
    fresh_scale = jnp.exp(fresh_peak - top)
    own_scale = jnp.exp(own_peak - top)
    scales = [jnp.exp(peak - top) for peak in peaks]
    denominator = fresh_scale * fresh_total + own_scale * own_total
    for scale, total in zip(scales, totals):
        denominator = denominator + scale * total
    numerator = fresh_scale * fresh_sum + own_scale * own_sum
    drain(sums_in.at[pl.ds(3, 2)], s4_recv.at[4])
    for k in range(2):
        numerator = numerator + scales[k] * sums_in[3 + k].astype(F32)
    inverse = 1.0 / denominator
    for h, lanes in enumerate(HALVES):
        cut = slice(lanes.start, lanes.start + lanes.size)
        piece = numerator[:, cut]
        drain(sums_in.at[pl.ds(5, 2), :, lanes], s4_recv.at[5 + h])
        for n in range(2):
            piece = piece + scales[2 + n] * sums_in[5 + n, :, cut].astype(F32)
        out[:, :, :, :, cut] = (piece * inverse).astype(BF16).reshape(2, 1, 2, 16, lanes.size)

    drain(outgoing.at[pl.ds(0, 7)], s1_send)
    drain(all_queries.at[pl.ds(0, 7)], q_send)
    for c in range(chunks):
        drain(gathered[c].at[pl.ds(0, 7)], s2_send.at[c])
        drain(picked[c].at[pl.ds(0, 7)], s3_send.at[c])
    drain(stats, st_send)
    drain(sums.at[pl.ds(0, 7)], s4_send)


def local(prefill_latent, stretch_page, page_table, page_list, lengths, queries, new_latent):
    vmem = pl.BlockSpec(memory_space=pltpu.VMEM)
    hbm = pl.BlockSpec(memory_space=pltpu.HBM)
    dma = pltpu.SemaphoreType.DMA
    chunks = len(CHUNKS)
    blocks = [pltpu.VMEM((8, 64, width), BF16) for _, width in CHUNKS]
    return pl.pallas_call(
        kernel,
        out_shape=(
            jax.ShapeDtypeStruct((2, 1, 2, 16, LAT), BF16),
            jax.ShapeDtypeStruct((8, 8, LATW), BF16),
        ),
        in_specs=[hbm] * 8,
        out_specs=(vmem, vmem),
        scratch_shapes=[
            pltpu.VMEM((8, 16, LATW), BF16),
            pltpu.SMEM((512,), I32),
            pltpu.VMEM((1, 512), I32),
            pltpu.VMEM((2, 512), I32),
            pltpu.SMEM((8, 64), I32),
            pltpu.SMEM((64,), I32),
            pltpu.VMEM((2, 1, 2, LATW), BF16),
            pltpu.VMEM((8, 16, 384), BF16),
            pltpu.VMEM((8, 16, 384), BF16),
            pltpu.VMEM((8, 2, 2, 16, LATW), BF16),
            pltpu.VMEM((512, 512), BF16),
            pltpu.VMEM((8, 64, LAT), BF16),
            pltpu.VMEM((8, 64, LAT), BF16),
            pltpu.VMEM((8, 8, 128), F32),
            pltpu.VMEM((8, 8, 128), F32),
            dma((8,)), dma, dma, dma((chunks,)), dma((chunks, 3)),
            dma((chunks,)), dma((chunks,)), dma, dma, dma, dma((7,)), dma,
            *blocks, *blocks, *blocks,
        ],
        compiler_params=pltpu.CompilerParams(
            collective_id=0, has_side_effects=True, vmem_limit_bytes=24 * 1024 * 1024
        ),
        name="place_and_attend",
    )(*[pltpu.with_memory_space_constraint(x, pltpu.HBM) for x in (
        prefill_latent, stretch_page, stretch_page.reshape(1, 512), page_table.T, page_list, lengths,
        queries, new_latent)]
    )


def solution(mesh):
    in_specs = (
        P("pages", None, None),
        P(),
        P(),
        P(),
        P(),
        P(None, "pages", None, "heads", None),
        P(None, "pages", None, None),
    )
    out_specs = (P(None, "pages", None, "heads", None), P("pages", "heads", None))
    return jax.shard_map(local, mesh=mesh, in_specs=in_specs, out_specs=out_specs, check_vma=False)
```
